32 devices in a mesh: dp: 4 (over x, core), prec: 4 (over z), pair: 2 (over y).
Axes of the slice: x: 2, y: 2, z: 4, core: 2. Of those that a mesh axis runs over, the one named last changes fastest.
Arguments:
- activations: bfloat16 [1024, 4096], P('dp', 'prec')
- output_grads: bfloat16 [1024, 16384], P('dp', 'pair')
- iter_counts: int32 [32, 8], P(('pair', 'dp'), 'prec'), may hold values from 1 to 2, as said below
Outputs:
- preconditioned: float32 [16384, 4096], P(('pair', 'dp'), 'prec')
The draws below stay inside these ranges and needn't reach their ends.
Inputs may be any that keep to these rules, and one draw needn't show every extreme that they name: `iter_counts`: newton iterations of each block; 2 is taken by at least one block in every draw.
All inputs are finite; a program needn't handle non-finite values.
Results may differ from the reference program's by a relative error of at most 0.0003.
Values may be sent and summed in bfloat16 or wider, within the bound.
A program may use at most 128 MiB of HBM per device.

```python
import math
import jax
import jax.numpy as jnp
from jax import lax

D = 4096
FF = 16384
BLK = 512
ITERS = 2
TOKENS = 1024


def feature_scales(key, width):
    jitter = jnp.exp(jax.random.uniform(key, (width,), minval=0.0, maxval=math.log(10.0)))
    incline = jnp.exp(jnp.arange(width, dtype=jnp.float32) * (math.log(3.0) / width))
    return jitter * incline / 8.9


def scaled_values(key, rows_total, width, spread):
    first, second = jax.random.split(key, 2)
    scales = feature_scales(first, width) * spread
    values = jax.random.normal(second, (rows_total, width)) * scales
    return values


def draw_activations(key, part):
    key = jax.random.fold_in(key, 1)
    return scaled_values(key, TOKENS, D, 1.0).astype(jnp.bfloat16)


def draw_output_grads(key, part):
    key = jax.random.fold_in(key, 2)
    return scaled_values(key, TOKENS, FF, 1.0 / math.sqrt(TOKENS)).astype(jnp.bfloat16)


def draw_iter_counts(key, part):
    key = jax.random.fold_in(key, 3)
    first, second = jax.random.split(key)
    shape = (FF // BLK, D // BLK)
    lottery = jax.random.randint(first, shape, 0, 16)
    plan = jnp.where(lottery == 0, ITERS, 1)
    chosen = jax.random.randint(second, (), 0, shape[0] * shape[1])
    places = jnp.arange(shape[0] * shape[1], dtype=jnp.int32).reshape(shape)
    return jnp.where(places == chosen, ITERS, plan).astype(jnp.int32)


def setup_inputs(seed: int = 0) -> dict:
    streams_of = jax.random.split(jax.random.key(seed), 4)
    activations = draw_activations(jax.random.fold_in(streams_of[3], 71), 0)
    output_grads = draw_output_grads(jax.random.fold_in(streams_of[3], 71), 0)
    iter_counts = draw_iter_counts(jax.random.fold_in(streams_of[3], 71), 0)
    return dict(activations=activations, output_grads=output_grads, iter_counts=iter_counts)


SHIFT = 0.001

def product(left, right):
    return jnp.dot(left, right, precision=lax.Precision.HIGHEST)

def inverse_root(statistic, plan):
    extent = statistic.shape[0]
    identity = jnp.eye(extent, dtype=statistic.dtype)
    shifted = statistic + SHIFT * identity
    scaling = 2.5 / jnp.sqrt(jnp.sum(shifted * shifted) + 1e-06)
    inverse = identity * jnp.sqrt(jnp.sqrt(scaling))
    coupled = shifted * scaling

    def advance(step_index, state_pair):
        current, matrix = state_pair
        factor = 1.25 * identity - 0.25 * matrix
        square = product(factor, factor)
        return (product(current, factor), product(product(square, square), matrix))
    inverse, coupled = lax.fori_loop(0, plan, advance, (inverse, coupled))
    return inverse

def precondition(block, plan):
    left_root = inverse_root(product(block, block.T), plan)
    right_root = inverse_root(product(block.T, block), plan)
    return product(product(left_root, block), right_root)

def reference(activations, output_grads, iter_counts):
    grad = jnp.dot(output_grads.T, activations, preferred_element_type=jnp.float32)
    ff_blocks = FF // BLK
    d_blocks = D // BLK
    blocks = grad.reshape(ff_blocks, BLK, d_blocks, BLK).transpose(0, 2, 1, 3).reshape(ff_blocks * d_blocks, BLK, BLK)
    updates = lax.map(lambda item: precondition(item[0], item[1]), (blocks, iter_counts.reshape(-1)))
    graft_ratio = jnp.sqrt(jnp.sum(grad * grad) / jnp.sum(updates * updates))
    scaled = updates * graft_ratio
    return scaled.reshape(ff_blocks, d_blocks, BLK, BLK).transpose(0, 2, 1, 3).reshape(FF, D)
```

```python
import functools
import jax
import jax.numpy as jnp
from jax import lax
from jax.experimental import pallas as pl
from jax.experimental.pallas import tpu as pltpu
from jax.sharding import PartitionSpec as P

BLK = 512
SHIFT = 0.001
NN = (((1,), (0,)), ((), ()))
NT = (((1,), (1,)), ((), ()))
TN = (((0,), (0,)), ((), ()))


def halves(x):
    high = x.astype(jnp.bfloat16)
    low = (x - high.astype(jnp.float32)).astype(jnp.bfloat16)
    return high, low


def dot(a, b, dims):
    return lax.dot_general(a, b, dims, preferred_element_type=jnp.float32)


def product(a, b, dims=NN):
    return dot(a[0], b[0], dims) + (dot(a[0], b[1], dims) + dot(a[1], b[0], dims))


def total(x):
    return jnp.sum(x, keepdims=True)


def first_iteration(g):
    gs = halves(g)
    left = product(gs, gs, NT)
    trace = total(g * g)
    norm = total(left * left) + (2.0 * SHIFT) * trace + BLK * SHIFT * SHIFT
    scaling = 2.5 / jnp.sqrt(norm + 1e-06)
    a = 1.25 - (0.25 * SHIFT) * scaling
    b = 0.25 * scaling
    ls = halves(left)
    half = a * g - b * product(ls, gs)
    update = (a * half - b * product(ls, halves(half))) * jnp.sqrt(scaling)
    return left, scaling, trace, update


def identity():
    rows = lax.broadcasted_iota(jnp.int32, (BLK, BLK), 0)
    return (rows == lax.broadcasted_iota(jnp.int32, (BLK, BLK), 1)).astype(jnp.float32)


def later_iterations(count, coupled_ref, update_ref):
    def advance(_, carry):
        coupled = coupled_ref[...]
        factor = halves(1.25 * identity() - 0.25 * coupled)
        square = halves(product(factor, factor))
        fourth = halves(product(square, square))
        coupled = product(fourth, halves(coupled))
        coupled_ref[...] = coupled
        factor = halves(1.25 * identity() - 0.25 * coupled)
        once = product(factor, halves(update_ref[...]))
        update_ref[...] = product(factor, halves(once))
        return carry

    lax.fori_loop(1, count, advance, 0)


def block_kernel(counts_ref, og_ref, act_ref, update_ref, squares_ref, coupled_ref):
    i, j = pl.program_id(0), pl.program_id(1)

    @pl.when((i == 0) & (j == 0))
    def _():
        squares_ref[...] = jnp.zeros_like(squares_ref)

    g = dot(og_ref[...], act_ref[...], TN)
    left, scaling, trace, update = first_iteration(g)
    update_ref[...] = update
    count = counts_ref[i, j]

    @pl.when(count > 1)
    def _():
        coupled_ref[...] = scaling * (left + SHIFT * identity())
        later_iterations(count, coupled_ref, update_ref)

    u = update_ref[...]
    squares_ref[0:8, :] += jnp.broadcast_to(trace, (8, 128))
    squares_ref[8:16, :] += jnp.broadcast_to(total(u * u), (8, 128))


def local_updates(og, act, counts):
    tokens, rows = og.shape
    features = act.shape[1]
    grid = (rows // BLK, features // BLK)
    return pl.pallas_call(
        block_kernel,
        grid=grid,
        in_specs=[
            pl.BlockSpec(memory_space=pltpu.SMEM),
            pl.BlockSpec((tokens, BLK), lambda i, j: (0, i)),
            pl.BlockSpec((tokens, BLK), lambda i, j: (0, j)),
        ],
        out_specs=[
            pl.BlockSpec((BLK, BLK), lambda i, j: (i, j)),
            pl.BlockSpec((16, 128), lambda i, j: (0, 0)),
        ],
        out_shape=[
            jax.ShapeDtypeStruct((rows, features), jnp.float32),
            jax.ShapeDtypeStruct((16, 128), jnp.float32),
        ],
        scratch_shapes=[pltpu.VMEM((BLK, BLK), jnp.float32)],
        compiler_params=pltpu.CompilerParams(vmem_limit_bytes=48 * 2**20),
    )(counts, og, act)


def per_device(activations, output_grads, iter_counts):
    act = lax.all_gather(activations, "dp", axis=0, tiled=True)
    og = lax.all_to_all(output_grads, "dp", split_axis=1, concat_axis=0, tiled=True)
    updates, squares = local_updates(og, act, iter_counts)
    sums = lax.psum(squares, ("dp", "prec", "pair"))
    return updates * jnp.sqrt(sums[0, 0] / sums[8, 0])


def solution(mesh):
    in_specs = (P("dp", "prec"), P("dp", "pair"), P(("pair", "dp"), "prec"))
    out_specs = P(("pair", "dp"), "prec")
    return jax.shard_map(
        per_device, mesh=mesh, in_specs=in_specs, out_specs=out_specs, check_vma=False
    )
```

```python
import functools
import jax
import jax.numpy as jnp
from jax import lax
from jax.experimental import pallas as pl
from jax.experimental.pallas import tpu as pltpu
from jax.sharding import PartitionSpec as P

BLK = 512
SHIFT = 0.001
NN = (((1,), (0,)), ((), ()))
NT = (((1,), (1,)), ((), ()))
TN = (((0,), (0,)), ((), ()))


def halves(x):
    high = x.astype(jnp.bfloat16)
    low = (x - high.astype(jnp.float32)).astype(jnp.bfloat16)
    return high, low


def dot(a, b, dims):
    return lax.dot_general(a, b, dims, preferred_element_type=jnp.float32)


def product(a, b, dims=NN):
    return dot(a[0], b[0], dims) + (dot(a[0], b[1], dims) + dot(a[1], b[0], dims))


def total(x):
    return jnp.sum(x, keepdims=True)


def first_iteration(g):
    gs = halves(g)
    left = product(gs, gs, NT)
    trace = total(g * g)
    norm = total(left * left) + (2.0 * SHIFT) * trace + BLK * SHIFT * SHIFT
    scaling = 2.5 / jnp.sqrt(norm + 1e-06)
    a = 1.25 - (0.25 * SHIFT) * scaling
    b = 0.25 * scaling
    ls = halves(left)
    half = a * g - b * product(ls, gs)
    update = (a * half - b * product(ls, halves(half))) * jnp.sqrt(scaling)
    return left, scaling, trace, update


def identity():
    rows = lax.broadcasted_iota(jnp.int32, (BLK, BLK), 0)
    return (rows == lax.broadcasted_iota(jnp.int32, (BLK, BLK), 1)).astype(jnp.float32)


def later_iterations(count, coupled_ref, update_ref):
    def advance(_, carry):
        coupled = coupled_ref[...]
        factor = halves(1.25 * identity() - 0.25 * coupled)
        square = halves(product(factor, factor))
        fourth = halves(product(square, square))
        coupled = product(fourth, halves(coupled))
        coupled_ref[...] = coupled
        factor = halves(1.25 * identity() - 0.25 * coupled)
        once = product(factor, halves(update_ref[...]))
        update_ref[...] = product(factor, halves(once))
        return carry

    lax.fori_loop(1, count, advance, 0)


def block_kernel(counts_ref, og_ref, act_ref, update_ref, squares_ref, coupled_ref):
    i, j = pl.program_id(0), pl.program_id(1)

    @pl.when((i == 0) & (j == 0))
    def _():
        squares_ref[...] = jnp.zeros_like(squares_ref)

    g = dot(og_ref[...], act_ref[...], TN)
    left, scaling, trace, update = first_iteration(g)
    update_ref[...] = update
    count = counts_ref[i, j]

    @pl.when(count > 1)
    def _():
        coupled_ref[...] = scaling * (left + SHIFT * identity())
        later_iterations(count, coupled_ref, update_ref)

    u = update_ref[...]
    squares_ref[0:8, :] += jnp.broadcast_to(trace, (8, 128))
    squares_ref[8:16, :] += jnp.broadcast_to(total(u * u), (8, 128))


def local_updates(og, act, counts):
    tokens, rows = og.shape
    features = act.shape[1]
    grid = (rows // BLK, features // BLK)
    return pl.pallas_call(
        block_kernel,
        grid=grid,
        in_specs=[
            pl.BlockSpec(memory_space=pltpu.SMEM),
            pl.BlockSpec((tokens, BLK), lambda i, j: (0, i)),
            pl.BlockSpec((tokens, BLK), lambda i, j: (0, j)),
        ],
        out_specs=[
            pl.BlockSpec((BLK, BLK), lambda i, j: (i, j)),
            pl.BlockSpec((16, 128), lambda i, j: (0, 0)),
        ],
        out_shape=[
            jax.ShapeDtypeStruct((rows, features), jnp.float32),
            jax.ShapeDtypeStruct((16, 128), jnp.float32),
        ],
        scratch_shapes=[pltpu.VMEM((BLK, BLK), jnp.float32)],
        compiler_params=pltpu.CompilerParams(vmem_limit_bytes=48 * 2**20),
    )(counts, og, act)


def remote(src, dst, send, recv, **device):
    return pltpu.make_async_remote_copy(
        src_ref=src, dst_ref=dst, send_sem=send, recv_sem=recv,
        device_id=device, device_id_type=pl.DeviceIdType.MESH,
    )


def gather_kernel(
    og_ref, act_ref, update_ref, left_ref, stats_ref,
    og_all, act_all, update_all, left_all,
    og_own, og_cs, og_cr, og_xs, og_xr, og_zs, og_zr,
    act_own, act_cs, act_cr, act_xs, act_xr, act_ys, act_yr, act_fs, act_fr,
    update_sem, left_sem,
):
    shard = og_ref.shape[0]
    half = shard // 2
    chunks, features = og_all.shape[0], act_all.shape[0]
    width = chunks * BLK
    me, z, y = lax.axis_index("dp"), lax.axis_index("prec"), lax.axis_index("pair")
    x, core = lax.div(me, 2), lax.rem(me, 2)
    mate, over, base = me + 1 - 2 * core, me + 2 - 4 * x, 2 - 2 * x
    over_mate = base + 1 - core
    side = lax.rem(z, 2)
    z_mate, y_mate = z + 1 - 2 * side, 1 - y

    def span(start, size):
        return pl.ds(pl.multiple_of(start, 128), size)

    def og_columns(device, a):
        return span(device * width + a * BLK, BLK)

    def og_rows(a, device, part):
        return og_all.at[a, span(device * shard + part * half, half)]

    def act_rows(j, device, part):
        return act_all.at[j, span(device * shard + part * half, half)]

    def own_og(a):
        return pltpu.make_async_copy(
            og_ref.at[:, og_columns(me, a)], og_all.at[a, span(me * shard, shard)], og_own.at[a]
        )

    def own_act(j):
        return pltpu.make_async_copy(
            act_ref.at[:, pl.ds(j * BLK, BLK)], act_all.at[j, span(me * shard, shard)], act_own.at[j]
        )

    def core_og(a):
        return remote(
            og_ref.at[:, og_columns(mate, a)], og_all.at[a, span(me * shard, shard)],
            og_cs.at[a], og_cr.at[a], dp=mate,
        )

    def core_act(j):
        return remote(
            act_ref.at[:, pl.ds(j * BLK, BLK)], act_all.at[j, span(me * shard, shard)],
            act_cs.at[j], act_cr.at[j], dp=mate,
        )

    def x_og(a, k):
        return remote(
            og_ref.at[span(side * half, half), og_columns(base + k, a)], og_rows(a, me, side),
            og_xs.at[a, k], og_xr.at[a, core], dp=base + k,
        )

    def x_og_arrived(a, k):
        there = og_rows(a, base + k, side)
        remote(there, there, og_xs.at[a, k], og_xr.at[a, k], dp=base + k).wait_recv()

    def z_og(a, k):
        there = og_rows(a, base + k, side)
        return remote(there, there, og_zs.at[a, k], og_zr.at[a, k], prec=z_mate)

    def x_act(j):
        return remote(
            act_ref.at[span(y * half, half), pl.ds(j * BLK, BLK)], act_rows(j, me, y),
            act_xs.at[j], act_xr.at[j], dp=over,
        )

    def y_act(j):
        there = act_rows(j, over, y)
        return remote(there, there, act_ys.at[j], act_yr.at[j], pair=y_mate)

    def f_act(j, k):
        there = act_rows(j, over, y if k == 0 else y_mate)
        return remote(there, there, act_fs.at[j, k], act_fr.at[j, k], dp=mate)

    barrier = pltpu.get_barrier_semaphore()
    for device in (dict(dp=mate), dict(dp=base), dict(dp=base + 1), dict(prec=z_mate), dict(pair=y_mate)):
        pl.semaphore_signal(barrier, inc=1, device_id=device, device_id_type=pl.DeviceIdType.MESH)
    pl.semaphore_wait(barrier, 5)

    def send_x(a):
        x_og(a, 0).start()
        x_og(a, 1).start()

    def pass_on_og(a):
        for k in range(2):
            x_og_arrived(a, k)
            z_og(a, k).start()

    def pass_on_act(j):
        x_act(j).wait_recv()
        y_act(j).start()
        f_act(j, 0).start()

    def pass_on_act_again(j):
        y_act(j).wait_recv()
        f_act(j, 1).start()

    x_act(0).start()
    send_x(0)
    for j in range(1, features):
        x_act(j).start()
    if chunks > 1:
        send_x(1)
    for j in range(features):
        core_act(j).start()
        own_act(j).start()
    for a in range(chunks):
        core_og(a).start()
        own_og(a).start()
    pass_on_act(0)
    pass_on_og(0)
    if chunks > 2:
        send_x(2)
    pass_on_act_again(0)
    for j in range(1, features):
        pass_on_act(j)
    for j in range(1, features):
        pass_on_act_again(j)
    for j in range(features):
        own_act(j).wait()
        core_act(j).wait_recv()
        f_act(j, 0).wait_recv()
        f_act(j, 1).wait_recv()

    def outgoing(s):
        a, j = lax.div(s, features), lax.rem(s, features)
        place = update_ref.at[span(a * BLK, BLK), span(j * BLK, BLK)]
        return (
            pltpu.make_async_copy(update_all.at[s], place, update_sem.at[s]),
            pltpu.make_async_copy(left_all.at[s], left_ref.at[s], left_sem.at[s]),
        )

    def step(s, carry):
        a, j = lax.div(s, features), lax.rem(s, features)

        @pl.when(j == 0)
        def _():
            own_og(a).wait()
            core_og(a).wait_recv()
            z_og(a, 0).wait_recv()
            z_og(a, 1).wait_recv()

        g = dot(og_all[a], act_all[j], TN)
        left, scaling, trace, update = first_iteration(g)
        update_all[s] = update
        left_all[s] = left
        for copy in outgoing(s):
            copy.start()
        stats_ref[s, 0:1, :] = jnp.broadcast_to(trace, (1, 128))
        stats_ref[s, 1:2, :] = jnp.broadcast_to(total(update * update), (1, 128))
        stats_ref[s, 2:3, :] = jnp.broadcast_to(scaling, (1, 128))
        stats_ref[s, 3:8, :] = jnp.zeros((5, 128), jnp.float32)

        @pl.when((j == 0) & (a + 1 < chunks))
        def _():
            pass_on_og(a + 1)

        @pl.when((j == 0) & (a + 3 < chunks))
        def _():
            send_x(a + 3)

        return carry

    lax.fori_loop(0, chunks * features, step, 0)

    for a in range(chunks):
        core_og(a).wait_send()
        for k in range(2):
            x_og(a, k).wait_send()
            z_og(a, k).wait_send()
    for j in range(features):
        core_act(j).wait_send()
        x_act(j).wait_send()
        y_act(j).wait_send()
        f_act(j, 0).wait_send()
        f_act(j, 1).wait_send()
    for s in range(chunks * features):
        for copy in outgoing(s):
            copy.wait()


def gathered_updates(og, act):
    shard, rows = og.shape[0], og.shape[1] // lax.axis_size("dp")
    tokens, width = shard * lax.axis_size("dp"), act.shape[1]
    chunks, features = rows // BLK, width // BLK
    blocks = chunks * features
    anywhere = pl.BlockSpec(memory_space=pl.ANY)
    one = pltpu.SemaphoreType.DMA((chunks,))
    two = pltpu.SemaphoreType.DMA((chunks, 2))
    act_one = pltpu.SemaphoreType.DMA((features,))
    act_two = pltpu.SemaphoreType.DMA((features, 2))
    return pl.pallas_call(
        gather_kernel,
        in_specs=[anywhere, anywhere],
        out_specs=[anywhere, anywhere, pl.BlockSpec(memory_space=pltpu.VMEM)],
        out_shape=[
            jax.ShapeDtypeStruct((rows, width), jnp.float32),
            jax.ShapeDtypeStruct((blocks, BLK, BLK), jnp.float32),
            jax.ShapeDtypeStruct((blocks, 8, 128), jnp.float32),
        ],
        scratch_shapes=[
            pltpu.VMEM((chunks, tokens, BLK), jnp.bfloat16),
            pltpu.VMEM((features, tokens, BLK), jnp.bfloat16),
            pltpu.VMEM((blocks, BLK, BLK), jnp.float32),
            pltpu.VMEM((blocks, BLK, BLK), jnp.float32),
            one, one, one, two, two, two, two,
            act_one, act_one, act_one, act_one, act_one, act_one, act_one, act_two, act_two,
            pltpu.SemaphoreType.DMA((blocks,)),
            pltpu.SemaphoreType.DMA((blocks,)),
        ],
        compiler_params=pltpu.CompilerParams(
            collective_id=0, has_side_effects=True, vmem_limit_bytes=56 * 2**20
        ),
    )(og, act)


def finish_kernel(counts_ref, stats_ref, left_ref, update_in, update_ref, squares_ref, coupled_ref, block_ref, sem):
    del update_in
    features = counts_ref.shape[1]
    squares_ref[...] = jnp.zeros_like(squares_ref)

    def step(s, carry):
        a, j = lax.div(s, features), lax.rem(s, features)
        count = counts_ref[a, j]
        squares_ref[0:8, :] += jnp.broadcast_to(stats_ref[s, 0:1, :], (8, 128))

        @pl.when(count <= 1)
        def _():
            squares_ref[8:16, :] += jnp.broadcast_to(stats_ref[s, 1:2, :], (8, 128))

        @pl.when(count > 1)
        def _():
            place = update_ref.at[
                pl.ds(pl.multiple_of(a * BLK, BLK), BLK), pl.ds(pl.multiple_of(j * BLK, BLK), BLK)
            ]
            left_in = pltpu.make_async_copy(left_ref.at[s], coupled_ref, sem.at[0])
            block_in = pltpu.make_async_copy(place, block_ref, sem.at[1])
            left_in.start()
            block_in.start()
            left_in.wait()
            block_in.wait()
            coupled_ref[...] = stats_ref[s, 2:3, 0:1] * (coupled_ref[...] + SHIFT * identity())
            later_iterations(count, coupled_ref, block_ref)
            block_out = pltpu.make_async_copy(block_ref, place, sem.at[2])
            block_out.start()
            u = block_ref[...]
            squares_ref[8:16, :] += jnp.broadcast_to(total(u * u), (8, 128))
            block_out.wait()

        return carry

    lax.fori_loop(0, counts_ref.shape[0] * features, step, 0)


def finished_updates(counts, stats, left, updates):
    anywhere = pl.BlockSpec(memory_space=pl.ANY)
    vmem = pl.BlockSpec(memory_space=pltpu.VMEM)
    return pl.pallas_call(
        finish_kernel,
        in_specs=[pl.BlockSpec(memory_space=pltpu.SMEM), vmem, anywhere, anywhere],
        out_specs=[anywhere, vmem],
        out_shape=[
            jax.ShapeDtypeStruct(updates.shape, jnp.float32),
            jax.ShapeDtypeStruct((16, 128), jnp.float32),
        ],
        scratch_shapes=[
            pltpu.VMEM((BLK, BLK), jnp.float32),
            pltpu.VMEM((BLK, BLK), jnp.float32),
            pltpu.SemaphoreType.DMA((3,)),
        ],
        input_output_aliases={3: 0},
        compiler_params=pltpu.CompilerParams(vmem_limit_bytes=56 * 2**20),
    )(counts, stats, left, updates)


def ratio_kernel(axes, squares_ref, ratio_ref, *scratch):
    buffers, sends, recvs = scratch[0:3], scratch[3:6], scratch[6:9]
    barrier = pltpu.get_barrier_semaphore()
    partners = 0
    for name, size in axes:
        for step in range(1, size):
            other = lax.rem(lax.axis_index(name) + step, size)
            pl.semaphore_signal(
                barrier, inc=1, device_id={name: other}, device_id_type=pl.DeviceIdType.MESH
            )
            partners += 1
    pl.semaphore_wait(barrier, partners)
    sums = squares_ref[...]
    for (name, size), buffer, send, recv in zip(axes, buffers, sends, recvs):
        me = lax.axis_index(name)
        buffer[me] = sums
        copies = []
        for step in range(1, size):
            copy = remote(
                buffer.at[me], buffer.at[me], send.at[step - 1], recv.at[step - 1],
                **{name: lax.rem(me + step, size)},
            )
            copy.start()
            copies.append(copy)
        for copy in copies:
            copy.wait()
        sums = buffer[0]
        for i in range(1, size):
            sums = sums + buffer[i]
    ratio_ref[...] = jnp.sqrt(sums[0:8, :] / sums[8:16, :])


def graft_ratio(squares):
    axes = [(name, lax.axis_size(name)) for name in ("dp", "prec", "pair")]
    vmem = pl.BlockSpec(memory_space=pltpu.VMEM)
    sems = [pltpu.SemaphoreType.DMA((max(size - 1, 1),)) for _, size in axes]
    return pl.pallas_call(
        functools.partial(ratio_kernel, axes),
        in_specs=[vmem],
        out_specs=vmem,
        out_shape=jax.ShapeDtypeStruct((8, 128), jnp.float32),
        scratch_shapes=[pltpu.VMEM((size, 16, 128), jnp.float32) for _, size in axes] + sems + sems,
        compiler_params=pltpu.CompilerParams(collective_id=1, has_side_effects=True),
    )(squares)


def scale_kernel(ratio_ref, update_ref, out_ref):
    out_ref[...] = update_ref[...] * ratio_ref[0:1, 0:1]


def scaled_updates(ratio, updates):
    rows, width = updates.shape
    block = pl.BlockSpec((BLK // 2, width), lambda i: (i, 0))
    return pl.pallas_call(
        scale_kernel,
        grid=(rows // (BLK // 2),),
        in_specs=[pl.BlockSpec(memory_space=pltpu.VMEM), block],
        out_specs=block,
        out_shape=jax.ShapeDtypeStruct(updates.shape, jnp.float32),
        compiler_params=pltpu.CompilerParams(vmem_limit_bytes=48 * 2**20),
    )(ratio, updates)


def gathered_first(activations, output_grads, iter_counts):
    act = lax.all_gather(activations, "dp", axis=0, tiled=True)
    og = lax.all_to_all(output_grads, "dp", split_axis=1, concat_axis=0, tiled=True)
    return local_updates(og, act, iter_counts)


def per_device(activations, output_grads, iter_counts):
    sizes = [lax.axis_size(name) for name in ("dp", "prec", "pair")]
    if sizes[0] == 4 and sizes[1] % 2 == 0 and sizes[2] == 2:
        updates, left, stats = gathered_updates(output_grads, activations)
        updates, squares = finished_updates(iter_counts, stats, left, updates)
    else:
        updates, squares = gathered_first(activations, output_grads, iter_counts)
    return scaled_updates(graft_ratio(squares), updates)


def solution(mesh):
    in_specs = (P("dp", "prec"), P("dp", "pair"), P(("pair", "dp"), "prec"))
    out_specs = P(("pair", "dp"), "prec")
    return jax.shard_map(
        per_device, mesh=mesh, in_specs=in_specs, out_specs=out_specs, check_vma=False
    )
```

```python
import functools
import jax
import jax.numpy as jnp
from jax import lax
from jax.experimental import pallas as pl
from jax.experimental.pallas import tpu as pltpu
from jax.sharding import PartitionSpec as P

BLK = 512
SHIFT = 0.001
NN = (((1,), (0,)), ((), ()))
NT = (((1,), (1,)), ((), ()))
TN = (((0,), (0,)), ((), ()))


def halves(x):
    high = x.astype(jnp.bfloat16)
    low = (x - high.astype(jnp.float32)).astype(jnp.bfloat16)
    return high, low


def dot(a, b, dims):
    return lax.dot_general(a, b, dims, preferred_element_type=jnp.float32)


def product(a, b, dims=NN):
    return dot(a[0], b[0], dims) + (dot(a[0], b[1], dims) + dot(a[1], b[0], dims))


def total(x):
    return jnp.sum(x, keepdims=True)


def first_iteration(g):
    gs = halves(g)
    left = product(gs, gs, NT)
    trace = total(g * g)
    norm = total(left * left) + (2.0 * SHIFT) * trace + BLK * SHIFT * SHIFT
    scaling = 2.5 / jnp.sqrt(norm + 1e-06)
    a = 1.25 - (0.25 * SHIFT) * scaling
    b = 0.25 * scaling
    ls = halves(left)
    half = a * g - b * product(ls, gs)
    update = (a * half - b * product(ls, halves(half))) * jnp.sqrt(scaling)
    return left, scaling, trace, update


def identity():
    rows = lax.broadcasted_iota(jnp.int32, (BLK, BLK), 0)
    return (rows == lax.broadcasted_iota(jnp.int32, (BLK, BLK), 1)).astype(jnp.float32)


def later_iterations(count, coupled_ref, update_ref):
    def advance(_, carry):
        coupled = coupled_ref[...]
        factor = halves(1.25 * identity() - 0.25 * coupled)
        square = halves(product(factor, factor))
        fourth = halves(product(square, square))
        coupled = product(fourth, halves(coupled))
        coupled_ref[...] = coupled
        factor = halves(1.25 * identity() - 0.25 * coupled)
        once = product(factor, halves(update_ref[...]))
        update_ref[...] = product(factor, halves(once))
        return carry

    lax.fori_loop(1, count, advance, 0)


def block_kernel(counts_ref, og_ref, act_ref, update_ref, squares_ref, coupled_ref):
    i, j = pl.program_id(0), pl.program_id(1)

    @pl.when((i == 0) & (j == 0))
    def _():
        squares_ref[...] = jnp.zeros_like(squares_ref)

    g = dot(og_ref[...], act_ref[...], TN)
    left, scaling, trace, update = first_iteration(g)
    update_ref[...] = update
    count = counts_ref[i, j]

    @pl.when(count > 1)
    def _():
        coupled_ref[...] = scaling * (left + SHIFT * identity())
        later_iterations(count, coupled_ref, update_ref)

    u = update_ref[...]
    squares_ref[0:8, :] += jnp.broadcast_to(trace, (8, 128))
    squares_ref[8:16, :] += jnp.broadcast_to(total(u * u), (8, 128))


def local_updates(og, act, counts):
    tokens, rows = og.shape
    features = act.shape[1]
    grid = (rows // BLK, features // BLK)
    return pl.pallas_call(
        block_kernel,
        grid=grid,
        in_specs=[
            pl.BlockSpec(memory_space=pltpu.SMEM),
            pl.BlockSpec((tokens, BLK), lambda i, j: (0, i)),
            pl.BlockSpec((tokens, BLK), lambda i, j: (0, j)),
        ],
        out_specs=[
            pl.BlockSpec((BLK, BLK), lambda i, j: (i, j)),
            pl.BlockSpec((16, 128), lambda i, j: (0, 0)),
        ],
        out_shape=[
            jax.ShapeDtypeStruct((rows, features), jnp.float32),
            jax.ShapeDtypeStruct((16, 128), jnp.float32),
        ],
        scratch_shapes=[pltpu.VMEM((BLK, BLK), jnp.float32)],
        compiler_params=pltpu.CompilerParams(vmem_limit_bytes=48 * 2**20),
    )(counts, og, act)


def remote(src, dst, send, recv, **device):
    return pltpu.make_async_remote_copy(
        src_ref=src, dst_ref=dst, send_sem=send, recv_sem=recv,
        device_id=device, device_id_type=pl.DeviceIdType.MESH,
    )


def gather_kernel(
    og_ref, act_ref, update_ref, left_ref, stats_ref,
    og_all, act_all,
    og_own, og_cs, og_cr, og_xs, og_xr, og_zs, og_zr,
    act_own, act_cs, act_cr, act_xs, act_xr, act_ys, act_yr, act_fs, act_fr,
):
    shard = og_ref.shape[0]
    half = shard // 2
    chunks, features = og_all.shape[0], act_all.shape[0]
    width = chunks * BLK
    me, z, y = lax.axis_index("dp"), lax.axis_index("prec"), lax.axis_index("pair")
    x, core = lax.div(me, 2), lax.rem(me, 2)
    mate, over, base = me + 1 - 2 * core, me + 2 - 4 * x, 2 - 2 * x
    over_mate = base + 1 - core
    side = lax.rem(z, 2)
    z_mate, y_mate = z + 1 - 2 * side, 1 - y

    def span(start, size):
        return pl.ds(pl.multiple_of(start, 128), size)

    def og_columns(device, a):
        return span(device * width + a * BLK, BLK)

    def og_rows(a, device, part):
        return og_all.at[a, span(device * shard + part * half, half)]

    def act_rows(j, device, part):
        return act_all.at[j, span(device * shard + part * half, half)]

    def own_og(a):
        return pltpu.make_async_copy(
            og_ref.at[:, og_columns(me, a)], og_all.at[a, span(me * shard, shard)], og_own.at[a]
        )

    def own_act(j):
        return pltpu.make_async_copy(
            act_ref.at[:, pl.ds(j * BLK, BLK)], act_all.at[j, span(me * shard, shard)], act_own.at[j]
        )

    def core_og(a):
        return remote(
            og_ref.at[:, og_columns(mate, a)], og_all.at[a, span(me * shard, shard)],
            og_cs.at[a], og_cr.at[a], dp=mate,
        )

    def core_act(j):
        return remote(
            act_ref.at[:, pl.ds(j * BLK, BLK)], act_all.at[j, span(me * shard, shard)],
            act_cs.at[j], act_cr.at[j], dp=mate,
        )

    def x_og(a, k):
        return remote(
            og_ref.at[span(side * half, half), og_columns(base + k, a)], og_rows(a, me, side),
            og_xs.at[a, k], og_xr.at[a, core], dp=base + k,
        )

    def x_og_arrived(a, k):
        there = og_rows(a, base + k, side)
        remote(there, there, og_xs.at[a, k], og_xr.at[a, k], dp=base + k).wait_recv()

    def z_og(a, k):
        there = og_rows(a, base + k, side)
        return remote(there, there, og_zs.at[a, k], og_zr.at[a, k], prec=z_mate)

    def x_act(j):
        return remote(
            act_ref.at[span(y * half, half), pl.ds(j * BLK, BLK)], act_rows(j, me, y),
            act_xs.at[j], act_xr.at[j], dp=over,
        )

    def y_act(j):
        there = act_rows(j, over, y)
        return remote(there, there, act_ys.at[j], act_yr.at[j], pair=y_mate)

    def f_act(j, k):
        there = act_rows(j, over, y if k == 0 else y_mate)
        return remote(there, there, act_fs.at[j, k], act_fr.at[j, k], dp=mate)

    barrier = pltpu.get_barrier_semaphore()
    for device in (dict(dp=mate), dict(dp=base), dict(dp=base + 1), dict(prec=z_mate), dict(pair=y_mate)):
        pl.semaphore_signal(barrier, inc=1, device_id=device, device_id_type=pl.DeviceIdType.MESH)
    pl.semaphore_wait(barrier, 5)

    def send_x(a):
        x_og(a, 0).start()
        x_og(a, 1).start()

    def pass_on_og(a):
        for k in range(2):
            x_og_arrived(a, k)
            z_og(a, k).start()

    def pass_on_act(j):
        x_act(j).wait_recv()
        y_act(j).start()
        f_act(j, 0).start()

    def pass_on_act_again(j):
        y_act(j).wait_recv()
        f_act(j, 1).start()

    def send_local(a, j):
        if j < features:
            core_act(j).start()
            own_act(j).start()
        if a < chunks:
            core_og(a).start()
            own_og(a).start()

    x_og(0, 0).start()
    send_local(0, 0)
    x_og(0, 0).wait_send()
    x_og(0, 1).start()
    x_og_arrived(0, 0)
    z_og(0, 0).start()
    x_og(0, 1).wait_send()
    x_act(0).start()
    x_og_arrived(0, 1)
    z_og(0, 1).start()
    for j in range(features):
        x_act(j).wait_send()
        if j + 1 < features:
            x_act(j + 1).start()
        elif chunks > 1:
            send_x(1)
        pass_on_act(j)
        if j == 0:
            for n in range(1, max(chunks, features)):
                send_local(n, n)
        pass_on_act_again(j)
    for j in range(features):
        own_act(j).wait()
        core_act(j).wait_recv()
        f_act(j, 0).wait_recv()
        f_act(j, 1).wait_recv()

    def step(s, carry):
        a, j = lax.div(s, features), lax.rem(s, features)

        @pl.when((j == 0) & (a > 0) & (a + 1 < chunks))
        def _():
            pass_on_og(a + 1)

        @pl.when((j == 0) & (a > 0) & (a + 2 < chunks))
        def _():
            send_x(a + 2)

        @pl.when(j == 0)
        def _():
            own_og(a).wait()
            core_og(a).wait_recv()
            z_og(a, 0).wait_recv()
            z_og(a, 1).wait_recv()

        g = dot(og_all[a], act_all[j], TN)
        left, scaling, trace, update = first_iteration(g)
        update_ref[s] = update
        left_ref[s] = left
        stats_ref[s, 0:1, :] = jnp.broadcast_to(trace, (1, 128))
        stats_ref[s, 1:2, :] = jnp.broadcast_to(total(update * update), (1, 128))
        stats_ref[s, 2:3, :] = jnp.broadcast_to(scaling, (1, 128))
        stats_ref[s, 3:8, :] = jnp.zeros((5, 128), jnp.float32)

        @pl.when((s == 0) & (chunks > 1))
        def _():
            pass_on_og(1)

        @pl.when((s == 0) & (chunks > 2))
        def _():
            send_x(2)

        return carry

    lax.fori_loop(0, chunks * features, step, 0)

    for a in range(chunks):
        core_og(a).wait_send()
        for k in range(2):
            if a > 0:
                x_og(a, k).wait_send()
            z_og(a, k).wait_send()
    for j in range(features):
        core_act(j).wait_send()
        y_act(j).wait_send()
        f_act(j, 0).wait_send()
        f_act(j, 1).wait_send()


def gathered_updates(og, act):
    shard, rows = og.shape[0], og.shape[1] // lax.axis_size("dp")
    tokens, width = shard * lax.axis_size("dp"), act.shape[1]
    chunks, features = rows // BLK, width // BLK
    blocks = chunks * features
    anywhere = pl.BlockSpec(memory_space=pl.ANY)
    one = pltpu.SemaphoreType.DMA((chunks,))
    two = pltpu.SemaphoreType.DMA((chunks, 2))
    act_one = pltpu.SemaphoreType.DMA((features,))
    act_two = pltpu.SemaphoreType.DMA((features, 2))
    return pl.pallas_call(
        gather_kernel,
        in_specs=[anywhere, anywhere],
        out_specs=[pl.BlockSpec(memory_space=pltpu.VMEM)] * 3,
        out_shape=[
            pltpu.VMEM((blocks, BLK, BLK), jnp.float32),
            pltpu.VMEM((blocks, BLK, BLK), jnp.float32),
            pltpu.VMEM((blocks, 8, 128), jnp.float32),
        ],
        scratch_shapes=[
            pltpu.VMEM((chunks, tokens, BLK), jnp.bfloat16),
            pltpu.VMEM((features, tokens, BLK), jnp.bfloat16),
            one, one, one, two, two, two, two,
            act_one, act_one, act_one, act_one, act_one, act_one, act_one, act_two, act_two,
        ],
        compiler_params=pltpu.CompilerParams(
            collective_id=0, has_side_effects=True, vmem_limit_bytes=36 * 2**20
        ),
    )(og, act)


def finish_kernel(counts_ref, stats_ref, left_ref, update_in, update_ref, squares_ref, coupled_ref):
    del update_in
    features = counts_ref.shape[1]
    squares_ref[...] = jnp.zeros_like(squares_ref)

    def step(s, carry):
        a, j = lax.div(s, features), lax.rem(s, features)
        count = counts_ref[a, j]
        squares_ref[0:8, :] += jnp.broadcast_to(stats_ref[s, 0:1, :], (8, 128))

        @pl.when(count <= 1)
        def _():
            squares_ref[8:16, :] += jnp.broadcast_to(stats_ref[s, 1:2, :], (8, 128))

        @pl.when(count > 1)
        def _():
            coupled_ref[...] = stats_ref[s, 2:3, 0:1] * (left_ref[s] + SHIFT * identity())
            later_iterations(count, coupled_ref, update_ref.at[s])
            u = update_ref[s]
            squares_ref[8:16, :] += jnp.broadcast_to(total(u * u), (8, 128))

        return carry

    lax.fori_loop(0, counts_ref.shape[0] * features, step, 0)


def finished_updates(counts, stats, left, updates):
    vmem = pl.BlockSpec(memory_space=pltpu.VMEM)
    return pl.pallas_call(
        finish_kernel,
        in_specs=[pl.BlockSpec(memory_space=pltpu.SMEM), vmem, vmem, vmem],
        out_specs=[vmem, vmem],
        out_shape=[
            pltpu.VMEM(updates.shape, jnp.float32),
            pltpu.VMEM((16, 128), jnp.float32),
        ],
        scratch_shapes=[pltpu.VMEM((BLK, BLK), jnp.float32)],
        input_output_aliases={3: 0},
        compiler_params=pltpu.CompilerParams(vmem_limit_bytes=36 * 2**20),
    )(counts, stats, left, updates)


def ratio_kernel(axes, squares_ref, ratio_ref, *scratch):
    buffers, sends, recvs = scratch[0:3], scratch[3:6], scratch[6:9]
    barrier = pltpu.get_barrier_semaphore()
    partners = 0
    for name, size in axes:
        for step in range(1, size):
            other = lax.rem(lax.axis_index(name) + step, size)
            pl.semaphore_signal(
                barrier, inc=1, device_id={name: other}, device_id_type=pl.DeviceIdType.MESH
            )
            partners += 1
    pl.semaphore_wait(barrier, partners)
    sums = squares_ref[...]
    for (name, size), buffer, send, recv in zip(axes, buffers, sends, recvs):
        me = lax.axis_index(name)
        buffer[me] = sums
        copies = []
        for step in range(1, size):
            copy = remote(
                buffer.at[me], buffer.at[me], send.at[step - 1], recv.at[step - 1],
                **{name: lax.rem(me + step, size)},
            )
            copy.start()
            copies.append(copy)
        for copy in copies:
            copy.wait()
        sums = buffer[0]
        for i in range(1, size):
            sums = sums + buffer[i]
    ratio_ref[...] = jnp.sqrt(sums[0:8, :] / sums[8:16, :])


def graft_ratio(squares):
    axes = [(name, lax.axis_size(name)) for name in ("dp", "prec", "pair")]
    vmem = pl.BlockSpec(memory_space=pltpu.VMEM)
    sems = [pltpu.SemaphoreType.DMA((max(size - 1, 1),)) for _, size in axes]
    return pl.pallas_call(
        functools.partial(ratio_kernel, axes),
        in_specs=[vmem],
        out_specs=vmem,
        out_shape=jax.ShapeDtypeStruct((8, 128), jnp.float32),
        scratch_shapes=[pltpu.VMEM((size, 16, 128), jnp.float32) for _, size in axes] + sems + sems,
        compiler_params=pltpu.CompilerParams(collective_id=1, has_side_effects=True),
    )(squares)


def scale_kernel(ratio_ref, update_ref, out_ref):
    out_ref[...] = update_ref[...] * ratio_ref[0:1, 0:1]


def scaled_updates(ratio, updates):
    rows, width = updates.shape
    block = pl.BlockSpec((BLK // 2, width), lambda i: (i, 0))
    return pl.pallas_call(
        scale_kernel,
        grid=(rows // (BLK // 2),),
        in_specs=[pl.BlockSpec(memory_space=pltpu.VMEM), block],
        out_specs=block,
        out_shape=jax.ShapeDtypeStruct(updates.shape, jnp.float32),
        compiler_params=pltpu.CompilerParams(vmem_limit_bytes=48 * 2**20),
    )(ratio, updates)


def scale_blocks_kernel(ratio_ref, update_ref, out_ref, scaled, sem):
    features = out_ref.shape[1] // BLK

    def place(s):
        a, j = lax.div(s, features), lax.rem(s, features)
        there = out_ref.at[
            pl.ds(pl.multiple_of(a * BLK, BLK), BLK), pl.ds(pl.multiple_of(j * BLK, BLK), BLK)
        ]
        return pltpu.make_async_copy(scaled.at[s], there, sem.at[s])

    def scale(s, carry):
        scaled[s] = update_ref[s] * ratio_ref[0:1, 0:1]
        place(s).start()
        return carry

    def wait(s, carry):
        place(s).wait()
        return carry

    lax.fori_loop(0, scaled.shape[0], scale, 0)
    lax.fori_loop(0, scaled.shape[0], wait, 0)


def scaled_blocks(ratio, updates, shape):
    vmem = pl.BlockSpec(memory_space=pltpu.VMEM)
    return pl.pallas_call(
        scale_blocks_kernel,
        in_specs=[vmem, vmem],
        out_specs=pl.BlockSpec(memory_space=pl.ANY),
        out_shape=jax.ShapeDtypeStruct(shape, jnp.float32),
        scratch_shapes=[
            pltpu.VMEM(updates.shape, jnp.float32),
            pltpu.SemaphoreType.DMA((updates.shape[0],)),
        ],
        compiler_params=pltpu.CompilerParams(vmem_limit_bytes=36 * 2**20),
    )(ratio, updates)


def gathered_first(activations, output_grads, iter_counts):
    act = lax.all_gather(activations, "dp", axis=0, tiled=True)
    og = lax.all_to_all(output_grads, "dp", split_axis=1, concat_axis=0, tiled=True)
    return local_updates(og, act, iter_counts)


def per_device(activations, output_grads, iter_counts):
    sizes = [lax.axis_size(name) for name in ("dp", "prec", "pair")]
    if sizes[0] == 4 and sizes[1] % 2 == 0 and sizes[2] == 2:
        updates, left, stats = gathered_updates(output_grads, activations)
        updates, squares = finished_updates(iter_counts, stats, left, updates)
        shape = (output_grads.shape[1] // sizes[0], activations.shape[1])
        return scaled_blocks(graft_ratio(squares), updates, shape)
    updates, squares = gathered_first(activations, output_grads, iter_counts)
    return scaled_updates(graft_ratio(squares), updates)


def solution(mesh):
    in_specs = (P("dp", "prec"), P("dp", "pair"), P(("pair", "dp"), "prec"))
    out_specs = P(("pair", "dp"), "prec")
    return jax.shard_map(
        per_device, mesh=mesh, in_specs=in_specs, out_specs=out_specs, check_vma=False
    )
```

```python
import functools
import math
import jax
import jax.numpy as jnp
from jax import lax
from jax.experimental import pallas as pl
from jax.experimental.pallas import tpu as pltpu
from jax.sharding import PartitionSpec as P

BLK = 512
SHIFT = 0.001
NN = (((1,), (0,)), ((), ()))
NT = (((1,), (1,)), ((), ()))
TN = (((0,), (0,)), ((), ()))


def halves(x):
    high = x.astype(jnp.bfloat16)
    low = (x - high.astype(jnp.float32)).astype(jnp.bfloat16)
    return high, low


def dot(a, b, dims):
    return lax.dot_general(a, b, dims, preferred_element_type=jnp.float32)


def product(a, b, dims=NN):
    depth = dims[0][1][0]
    left = jnp.concatenate([a[0], a[0], a[1]], axis=1)
    return dot(left, jnp.concatenate([b[0], b[1], b[0]], axis=depth), dims)


def total(x):
    return jnp.sum(x, keepdims=True)


def first_iteration(g):
    gs = halves(g)
    left = product(gs, gs, NT)
    trace = total(g * g)
    norm = total(left * left) + (2.0 * SHIFT) * trace + BLK * SHIFT * SHIFT
    scaling = 2.5 / jnp.sqrt(norm + 1e-06)
    a = 1.25 - (0.25 * SHIFT) * scaling
    b = 0.25 * scaling
    ls = halves(left)
    half = a * g - b * product(ls, gs)
    update = (a * half - b * product(ls, halves(half))) * jnp.sqrt(scaling)
    return left, scaling, trace, update


def identity():
    rows = lax.broadcasted_iota(jnp.int32, (BLK, BLK), 0)
    return (rows == lax.broadcasted_iota(jnp.int32, (BLK, BLK), 1)).astype(jnp.float32)


def later_iterations(count, coupled_ref, update_ref):
    def advance(_, carry):
        coupled = coupled_ref[...]
        factor = halves(1.25 * identity() - 0.25 * coupled)
        square = halves(product(factor, factor))
        fourth = halves(product(square, square))
        coupled = product(fourth, halves(coupled))
        coupled_ref[...] = coupled
        factor = halves(1.25 * identity() - 0.25 * coupled)
        once = product(factor, halves(update_ref[...]))
        update_ref[...] = product(factor, halves(once))
        return carry

    lax.fori_loop(1, count, advance, 0)


def block_kernel(counts_ref, og_ref, act_ref, update_ref, squares_ref, coupled_ref):
    i, j = pl.program_id(0), pl.program_id(1)

    @pl.when((i == 0) & (j == 0))
    def _():
        squares_ref[...] = jnp.zeros_like(squares_ref)

    g = dot(og_ref[...], act_ref[...], TN)
    left, scaling, trace, update = first_iteration(g)
    update_ref[...] = update
    count = counts_ref[i, j]

    @pl.when(count > 1)
    def _():
        coupled_ref[...] = scaling * (left + SHIFT * identity())
        later_iterations(count, coupled_ref, update_ref)

    u = update_ref[...]
    squares_ref[0:8, :] += jnp.broadcast_to(trace, (8, 128))
    squares_ref[8:16, :] += jnp.broadcast_to(total(u * u), (8, 128))


def local_updates(og, act, counts):
    tokens, rows = og.shape
    features = act.shape[1]
    grid = (rows // BLK, features // BLK)
    return pl.pallas_call(
        block_kernel,
        grid=grid,
        in_specs=[
            pl.BlockSpec(memory_space=pltpu.SMEM),
            pl.BlockSpec((tokens, BLK), lambda i, j: (0, i)),
            pl.BlockSpec((tokens, BLK), lambda i, j: (0, j)),
        ],
        out_specs=[
            pl.BlockSpec((BLK, BLK), lambda i, j: (i, j)),
            pl.BlockSpec((16, 128), lambda i, j: (0, 0)),
        ],
        out_shape=[
            jax.ShapeDtypeStruct((rows, features), jnp.float32),
            jax.ShapeDtypeStruct((16, 128), jnp.float32),
        ],
        scratch_shapes=[pltpu.VMEM((BLK, BLK), jnp.float32)],
        compiler_params=pltpu.CompilerParams(vmem_limit_bytes=48 * 2**20),
    )(counts, og, act)


def remote(src, dst, send, recv, **device):
    return pltpu.make_async_remote_copy(
        src_ref=src, dst_ref=dst, send_sem=send, recv_sem=recv,
        device_id=device, device_id_type=pl.DeviceIdType.MESH,
    )


def gather_kernel(
    og_ref, act_ref, update_ref, left_ref, stats_ref,
    og_all, act_all,
    og_own, og_cs, og_cr, og_xs, og_xr, og_zs, og_zr,
    act_own, act_cs, act_cr, act_xs, act_xr, act_ys, act_yr, act_fs, act_fr,
):
    shard = og_ref.shape[0]
    half = shard // 2
    chunks, features = og_all.shape[0], act_all.shape[0]
    width = chunks * BLK
    me, z, y = lax.axis_index("dp"), lax.axis_index("prec"), lax.axis_index("pair")
    x, core = lax.div(me, 2), lax.rem(me, 2)
    mate, over, base = me + 1 - 2 * core, me + 2 - 4 * x, 2 - 2 * x
    over_mate = base + 1 - core
    side = lax.rem(z, 2)
    z_mate, y_mate = z + 1 - 2 * side, 1 - y

    def span(start, size):
        return pl.ds(pl.multiple_of(start, 128), size)

    def og_columns(device, a):
        return span(device * width + a * BLK, BLK)

    def og_rows(a, device, part):
        return og_all.at[a, span(device * shard + part * half, half)]

    def act_rows(j, device, part):
        return act_all.at[j, span(device * shard + part * half, half)]

    def own_og(a):
        return pltpu.make_async_copy(
            og_ref.at[:, og_columns(me, a)], og_all.at[a, span(me * shard, shard)], og_own.at[a]
        )

    def own_act(j):
        return pltpu.make_async_copy(
            act_ref.at[:, span(j * BLK, BLK)], act_all.at[j, span(me * shard, shard)], act_own.at[j]
        )

    def core_og(a):
        return remote(
            og_ref.at[:, og_columns(mate, a)], og_all.at[a, span(me * shard, shard)],
            og_cs.at[a], og_cr.at[a], dp=mate,
        )

    def core_act(j):
        return remote(
            act_ref.at[:, span(j * BLK, BLK)], act_all.at[j, span(me * shard, shard)],
            act_cs.at[j], act_cr.at[j], dp=mate,
        )

    def x_og(a, k):
        return remote(
            og_ref.at[span(side * half, half), og_columns(base + k, a)], og_rows(a, me, side),
            og_xs.at[a, k], og_xr.at[a, core], dp=base + k,
        )

    def x_og_arrived(a, k):
        there = og_rows(a, base + k, side)
        remote(there, there, og_xs.at[a, k], og_xr.at[a, k], dp=base + k).wait_recv()

    def z_og(a, k):
        there = og_rows(a, base + k, side)
        return remote(there, there, og_zs.at[a, k], og_zr.at[a, k], prec=z_mate)

    def x_act(j):
        return remote(
            act_ref.at[span(y * half, half), pl.ds(j * BLK, BLK)], act_rows(j, me, y),
            act_xs.at[j], act_xr.at[j], dp=over,
        )

    def y_act(j):
        there = act_rows(j, over, y)
        return remote(there, there, act_ys.at[j], act_yr.at[j], pair=y_mate)

    def f_act(j, k):
        there = act_rows(j, over, y if k == 0 else y_mate)
        return remote(there, there, act_fs.at[j, k], act_fr.at[j, k], dp=mate)

    barrier = pltpu.get_barrier_semaphore()
    for device in (dict(dp=mate), dict(dp=base), dict(dp=base + 1), dict(prec=z_mate), dict(pair=y_mate)):
        pl.semaphore_signal(barrier, inc=1, device_id=device, device_id_type=pl.DeviceIdType.MESH)
    pl.semaphore_wait(barrier, 5)

    def send_x(a):
        x_og(a, 0).start()
        x_og(a, 1).start()

    def pass_on_og(a):
        for k in range(2):
            x_og_arrived(a, k)
            z_og(a, k).start()

    def pass_on_act(j):
        x_act(j).wait_recv()
        y_act(j).start()
        f_act(j, 0).start()

    def pass_on_act_again(j):
        y_act(j).wait_recv()
        f_act(j, 1).start()

    def send_local(a, j):
        if j < features:
            core_act(j).start()
            own_act(j).start()
        if a < chunks:
            core_og(a).start()
            own_og(a).start()

    x_act(0).start()
    x_og(0, 0).start()
    send_local(0, 0)
    x_act(0).wait_send()
    x_og(0, 1).start()
    pass_on_act(0)
    x_og(0, 0).wait_send()
    if features > 1:
        x_act(1).start()
    x_og_arrived(0, 0)
    z_og(0, 0).start()
    pass_on_act_again(0)
    x_og(0, 1).wait_send()
    if chunks > 1:
        x_og(1, 0).start()
    x_og_arrived(0, 1)
    z_og(0, 1).start()
    for n in range(1, max(chunks, features)):
        send_local(n, n)
    for j in range(1, features):
        x_act(j).wait_send()
        if j + 1 < features:
            x_act(j + 1).start()
    if chunks > 1:
        x_og(1, 1).start()
    for j in range(1, features):
        pass_on_act(j)
        pass_on_act_again(j)

    def step(s, carry):
        a, j = lax.div(s, features), lax.rem(s, features)

        @pl.when((j == 0) & (a > 0) & (a + 1 < chunks))
        def _():
            pass_on_og(a + 1)

        @pl.when((j == 0) & (a > 0) & (a + 2 < chunks))
        def _():
            send_x(a + 2)

        @pl.when(j == 0)
        def _():
            own_og(a).wait()
            core_og(a).wait_recv()
            z_og(a, 0).wait_recv()
            z_og(a, 1).wait_recv()

        @pl.when(a == 0)
        def _():
            own_act(j).wait()
            core_act(j).wait_recv()
            f_act(j, 0).wait_recv()
            f_act(j, 1).wait_recv()

        g = dot(og_all[a], act_all[j], TN)
        left, scaling, trace, update = first_iteration(g)
        update_ref[s] = update
        left_ref[s] = left
        stats_ref[s, 0:1, :] = jnp.broadcast_to(trace, (1, 128))
        stats_ref[s, 1:2, :] = jnp.broadcast_to(total(update * update), (1, 128))
        stats_ref[s, 2:3, :] = jnp.broadcast_to(scaling, (1, 128))
        stats_ref[s, 3:8, :] = jnp.zeros((5, 128), jnp.float32)

        @pl.when((s == 0) & (chunks > 1))
        def _():
            pass_on_og(1)

        @pl.when((s == 0) & (chunks > 2))
        def _():
            send_x(2)

        return carry

    lax.fori_loop(0, chunks * features, step, 0)

    for a in range(chunks):
        core_og(a).wait_send()
        for k in range(2):
            if a > 0:
                x_og(a, k).wait_send()
            z_og(a, k).wait_send()
    for j in range(features):
        core_act(j).wait_send()
        y_act(j).wait_send()
        f_act(j, 0).wait_send()
        f_act(j, 1).wait_send()


def gathered_updates(og, act):
    shard, rows = og.shape[0], og.shape[1] // lax.axis_size("dp")
    tokens, width = shard * lax.axis_size("dp"), act.shape[1]
    chunks, features = rows // BLK, width // BLK
    blocks = chunks * features
    anywhere = pl.BlockSpec(memory_space=pl.ANY)
    one = pltpu.SemaphoreType.DMA((chunks,))
    two = pltpu.SemaphoreType.DMA((chunks, 2))
    act_one = pltpu.SemaphoreType.DMA((features,))
    act_two = pltpu.SemaphoreType.DMA((features, 2))
    return pl.pallas_call(
        gather_kernel,
        in_specs=[anywhere, anywhere],
        out_specs=[pl.BlockSpec(memory_space=pltpu.VMEM)] * 3,
        out_shape=[
            pltpu.VMEM((blocks, BLK, BLK), jnp.float32),
            pltpu.VMEM((blocks, BLK, BLK), jnp.float32),
            pltpu.VMEM((blocks, 8, 128), jnp.float32),
        ],
        scratch_shapes=[
            pltpu.VMEM((chunks, tokens, BLK), jnp.bfloat16),
            pltpu.VMEM((features, tokens, BLK), jnp.bfloat16),
            one, one, one, two, two, two, two,
            act_one, act_one, act_one, act_one, act_one, act_one, act_one, act_two, act_two,
        ],
        compiler_params=pltpu.CompilerParams(
            collective_id=0, has_side_effects=True, vmem_limit_bytes=36 * 2**20
        ),
    )(og, act)


def finish_kernel(counts_ref, stats_ref, left_ref, update_in, update_ref, squares_ref, coupled_ref):
    del update_in
    features = counts_ref.shape[1]
    squares_ref[...] = jnp.zeros_like(squares_ref)

    def step(s, carry):
        a, j = lax.div(s, features), lax.rem(s, features)
        count = counts_ref[a, j]
        squares_ref[0:8, :] += jnp.broadcast_to(stats_ref[s, 0:1, :], (8, 128))

        @pl.when(count <= 1)
        def _():
            squares_ref[8:16, :] += jnp.broadcast_to(stats_ref[s, 1:2, :], (8, 128))

        @pl.when(count > 1)
        def _():
            coupled_ref[...] = stats_ref[s, 2:3, 0:1] * (left_ref[s] + SHIFT * identity())
            later_iterations(count, coupled_ref, update_ref.at[s])
            u = update_ref[s]
            squares_ref[8:16, :] += jnp.broadcast_to(total(u * u), (8, 128))

        return carry

    lax.fori_loop(0, counts_ref.shape[0] * features, step, 0)


def finished_updates(counts, stats, left, updates):
    vmem = pl.BlockSpec(memory_space=pltpu.VMEM)
    return pl.pallas_call(
        finish_kernel,
        in_specs=[pl.BlockSpec(memory_space=pltpu.SMEM), vmem, vmem, vmem],
        out_specs=[vmem, vmem],
        out_shape=[
            pltpu.VMEM(updates.shape, jnp.float32),
            pltpu.VMEM((16, 128), jnp.float32),
        ],
        scratch_shapes=[pltpu.VMEM((BLK, BLK), jnp.float32)],
        input_output_aliases={3: 0},
        compiler_params=pltpu.CompilerParams(vmem_limit_bytes=36 * 2**20),
    )(counts, stats, left, updates)


def ratio_kernel(groups, squares_ref, ratio_ref, *scratch):
    count = len(groups)
    buffers, sends, recvs = scratch[:count], scratch[count:2 * count], scratch[2 * count:]

    def place(group):
        index = 0
        for name, size in group:
            index = index * size + lax.axis_index(name)
        return index

    def device(group, index):
        found = {}
        for name, size in reversed(group):
            found[name] = lax.rem(index, size)
            index = lax.div(index, size)
        return found

    barrier = pltpu.get_barrier_semaphore()
    partners = 0
    for group in groups:
        extent = math.prod(size for _, size in group)
        for step in range(1, extent):
            pl.semaphore_signal(
                barrier, inc=1, device_id=device(group, lax.rem(place(group) + step, extent)),
                device_id_type=pl.DeviceIdType.MESH,
            )
            partners += 1
    pl.semaphore_wait(barrier, partners)
    sums = squares_ref[...]
    for group, buffer, send, recv in zip(groups, buffers, sends, recvs):
        me, extent = place(group), buffer.shape[0]
        buffer[me] = sums
        copies = []
        for step in range(1, extent):
            copy = remote(
                buffer.at[me], buffer.at[me], send.at[step - 1], recv.at[step - 1],
                **device(group, lax.rem(me + step, extent)),
            )
            copy.start()
            copies.append(copy)
        for copy in copies:
            copy.wait()
        sums = buffer[0]
        for i in range(1, extent):
            sums = sums + buffer[i]
    ratio_ref[...] = jnp.sqrt(sums[0:8, :] / sums[8:16, :])


def graft_ratio(squares):
    sizes = {name: lax.axis_size(name) for name in ("dp", "prec", "pair")}
    groups = [[("dp", sizes["dp"])], [("prec", sizes["prec"]), ("pair", sizes["pair"])]]
    extents = [math.prod(size for _, size in group) for group in groups]
    vmem = pl.BlockSpec(memory_space=pltpu.VMEM)
    sems = [pltpu.SemaphoreType.DMA((max(extent - 1, 1),)) for extent in extents]
    return pl.pallas_call(
        functools.partial(ratio_kernel, groups),
        in_specs=[vmem],
        out_specs=vmem,
        out_shape=jax.ShapeDtypeStruct((8, 128), jnp.float32),
        scratch_shapes=[pltpu.VMEM((extent, 16, 128), jnp.float32) for extent in extents] + sems + sems,
        compiler_params=pltpu.CompilerParams(
            collective_id=1, has_side_effects=True, vmem_limit_bytes=8 * 2**20
        ),
    )(squares)


def scale_kernel(ratio_ref, update_ref, out_ref):
    out_ref[...] = update_ref[...] * ratio_ref[0:1, 0:1]


def scaled_updates(ratio, updates):
    rows, width = updates.shape
    block = pl.BlockSpec((BLK // 2, width), lambda i: (i, 0))
    return pl.pallas_call(
        scale_kernel,
        grid=(rows // (BLK // 2),),
        in_specs=[pl.BlockSpec(memory_space=pltpu.VMEM), block],
        out_specs=block,
        out_shape=jax.ShapeDtypeStruct(updates.shape, jnp.float32),
        compiler_params=pltpu.CompilerParams(vmem_limit_bytes=48 * 2**20),
    )(ratio, updates)


def scale_blocks_kernel(ratio_ref, update_ref, out_ref, scaled, sem):
    features = out_ref.shape[1] // BLK

    def place(s):
        a, j = lax.div(s, features), lax.rem(s, features)
        there = out_ref.at[
            pl.ds(pl.multiple_of(a * BLK, BLK), BLK), pl.ds(pl.multiple_of(j * BLK, BLK), BLK)
        ]
        return pltpu.make_async_copy(scaled.at[s], there, sem.at[s])

    def scale(s, carry):
        scaled[s] = update_ref[s] * ratio_ref[0:1, 0:1]
        place(s).start()
        return carry

    def wait(s, carry):
        place(s).wait()
        return carry

    lax.fori_loop(0, scaled.shape[0], scale, 0)
    lax.fori_loop(0, scaled.shape[0], wait, 0)


def scaled_blocks(ratio, updates, shape):
    vmem = pl.BlockSpec(memory_space=pltpu.VMEM)
    return pl.pallas_call(
        scale_blocks_kernel,
        in_specs=[vmem, vmem],
        out_specs=pl.BlockSpec(memory_space=pl.ANY),
        out_shape=jax.ShapeDtypeStruct(shape, jnp.float32),
        scratch_shapes=[
            pltpu.VMEM(updates.shape, jnp.float32),
            pltpu.SemaphoreType.DMA((updates.shape[0],)),
        ],
        compiler_params=pltpu.CompilerParams(vmem_limit_bytes=36 * 2**20),
    )(ratio, updates)


def gathered_first(activations, output_grads, iter_counts):
    act = lax.all_gather(activations, "dp", axis=0, tiled=True)
    og = lax.all_to_all(output_grads, "dp", split_axis=1, concat_axis=0, tiled=True)
    return local_updates(og, act, iter_counts)


def per_device(activations, output_grads, iter_counts):
    sizes = [lax.axis_size(name) for name in ("dp", "prec", "pair")]
    if sizes[0] == 4 and sizes[1] % 2 == 0 and sizes[2] == 2:
        updates, left, stats = gathered_updates(output_grads, activations)
        updates, squares = finished_updates(iter_counts, stats, left, updates)
        shape = (output_grads.shape[1] // sizes[0], activations.shape[1])
        return scaled_blocks(graft_ratio(squares), updates, shape)
    updates, squares = gathered_first(activations, output_grads, iter_counts)
    return scaled_updates(graft_ratio(squares), updates)


def solution(mesh):
    in_specs = (P("dp", "prec"), P("dp", "pair"), P(("pair", "dp"), "prec"))
    out_specs = P(("pair", "dp"), "prec")
    return jax.shard_map(
        per_device, mesh=mesh, in_specs=in_specs, out_specs=out_specs, check_vma=False
    )
```

```python
import functools
import math
import jax
import jax.numpy as jnp
from jax import lax
from jax.experimental import pallas as pl
from jax.experimental.pallas import tpu as pltpu
from jax.sharding import PartitionSpec as P

BLK = 512
SHIFT = 0.001
NN = (((1,), (0,)), ((), ()))
NT = (((1,), (1,)), ((), ()))
TN = (((0,), (0,)), ((), ()))


def halves(x):
    high = x.astype(jnp.bfloat16)
    low = (x - high.astype(jnp.float32)).astype(jnp.bfloat16)
    return high, low


def dot(a, b, dims):
    return lax.dot_general(a, b, dims, preferred_element_type=jnp.float32)


def product(a, b, dims=NN):
    depth = dims[0][1][0]
    left = jnp.concatenate([a[0], a[0], a[1]], axis=1)
    return dot(left, jnp.concatenate([b[0], b[1], b[0]], axis=depth), dims)


def total(x):
    return jnp.sum(x, keepdims=True)


def scaling_of(left, trace):
    norm = total(left * left) + (2.0 * SHIFT) * trace + BLK * SHIFT * SHIFT
    return 2.5 / jnp.sqrt(norm + 1e-06)


def factor_terms(scaling):
    return 1.25 - (0.25 * SHIFT) * scaling, 0.25 * scaling


def first_iteration(g):
    gs = halves(g)
    left = product(gs, gs, NT)
    trace = total(g * g)
    scaling = scaling_of(left, trace)
    main, slope = factor_terms(scaling)
    ls = halves(left)
    half = main * g - slope * product(ls, gs)
    update = (main * half - slope * product(ls, halves(half))) * jnp.sqrt(scaling)
    return left, scaling, trace, update


def identity():
    rows = lax.broadcasted_iota(jnp.int32, (BLK, BLK), 0)
    return (rows == lax.broadcasted_iota(jnp.int32, (BLK, BLK), 1)).astype(jnp.float32)


def later_iterations(count, coupled_ref, update_ref):
    def advance(_, carry):
        coupled = coupled_ref[...]
        factor = halves(1.25 * identity() - 0.25 * coupled)
        square = halves(product(factor, factor))
        fourth = halves(product(square, square))
        coupled = product(fourth, halves(coupled))
        coupled_ref[...] = coupled
        factor = halves(1.25 * identity() - 0.25 * coupled)
        once = product(factor, halves(update_ref[...]))
        update_ref[...] = product(factor, halves(once))
        return carry

    lax.fori_loop(1, count, advance, 0)


def block_kernel(counts_ref, og_ref, act_ref, update_ref, squares_ref, coupled_ref):
    i, j = pl.program_id(0), pl.program_id(1)

    @pl.when((i == 0) & (j == 0))
    def _():
        squares_ref[...] = jnp.zeros_like(squares_ref)

    g = dot(og_ref[...], act_ref[...], TN)
    left, scaling, trace, update = first_iteration(g)
    update_ref[...] = update
    count = counts_ref[i, j]

    @pl.when(count > 1)
    def _():
        coupled_ref[...] = scaling * (left + SHIFT * identity())
        later_iterations(count, coupled_ref, update_ref)

    u = update_ref[...]
    squares_ref[0:8, :] += jnp.broadcast_to(trace, (8, 128))
    squares_ref[8:16, :] += jnp.broadcast_to(total(u * u), (8, 128))


def local_updates(og, act, counts):
    tokens, rows = og.shape
    features = act.shape[1]
    grid = (rows // BLK, features // BLK)
    return pl.pallas_call(
        block_kernel,
        grid=grid,
        in_specs=[
            pl.BlockSpec(memory_space=pltpu.SMEM),
            pl.BlockSpec((tokens, BLK), lambda i, j: (0, i)),
            pl.BlockSpec((tokens, BLK), lambda i, j: (0, j)),
        ],
        out_specs=[
            pl.BlockSpec((BLK, BLK), lambda i, j: (i, j)),
            pl.BlockSpec((16, 128), lambda i, j: (0, 0)),
        ],
        out_shape=[
            jax.ShapeDtypeStruct((rows, features), jnp.float32),
            jax.ShapeDtypeStruct((16, 128), jnp.float32),
        ],
        scratch_shapes=[pltpu.VMEM((BLK, BLK), jnp.float32)],
        compiler_params=pltpu.CompilerParams(vmem_limit_bytes=48 * 2**20),
    )(counts, og, act)


def remote(src, dst, send, recv, **device):
    return pltpu.make_async_remote_copy(
        src_ref=src, dst_ref=dst, send_sem=send, recv_sem=recv,
        device_id=device, device_id_type=pl.DeviceIdType.MESH,
    )


def gather_kernel(
    og_ref, act_ref, update_ref, left_ref, stats_ref,
    og_all, act_all, g_parts, l_parts,
    og_own, og_cs, og_cr, og_xs, og_xr, og_zs, og_zr,
    act_own, act_cs, act_cr, act_xs, act_xr, act_ys, act_yr, act_fs, act_fr,
):
    shard = og_ref.shape[0]
    half = shard // 2
    chunks, features = og_all.shape[0], act_all.shape[0]
    width = chunks * BLK
    me, z, y = lax.axis_index("dp"), lax.axis_index("prec"), lax.axis_index("pair")
    x, core = lax.div(me, 2), lax.rem(me, 2)
    mate, over, base = me + 1 - 2 * core, me + 2 - 4 * x, 2 - 2 * x
    over_mate = base + 1 - core
    side = lax.rem(z, 2)
    z_mate, y_mate = z + 1 - 2 * side, 1 - y

    def span(start, size):
        return pl.ds(pl.multiple_of(start, 128), size)

    def og_columns(device, a):
        return span(device * width + a * BLK, BLK)

    def og_rows(a, device, part):
        return og_all.at[a, span(device * shard + part * half, half)]

    def act_rows(j, device, part):
        return act_all.at[j, span(device * shard + part * half, half)]

    def own_og(a):
        return pltpu.make_async_copy(
            og_ref.at[:, og_columns(me, a)], og_all.at[a, span(me * shard, shard)], og_own.at[a]
        )

    def own_act(j):
        return pltpu.make_async_copy(
            act_ref.at[:, span(j * BLK, BLK)], act_all.at[j, span(me * shard, shard)], act_own.at[j]
        )

    def core_og(a):
        return remote(
            og_ref.at[:, og_columns(mate, a)], og_all.at[a, span(me * shard, shard)],
            og_cs.at[a], og_cr.at[a], dp=mate,
        )

    def core_act(j):
        return remote(
            act_ref.at[:, span(j * BLK, BLK)], act_all.at[j, span(me * shard, shard)],
            act_cs.at[j], act_cr.at[j], dp=mate,
        )

    def x_og(a, k):
        return remote(
            og_ref.at[span(side * half, half), og_columns(base + k, a)], og_rows(a, me, side),
            og_xs.at[a, k], og_xr.at[a, core], dp=base + k,
        )

    def x_og_arrived(a, k):
        there = og_rows(a, base + k, side)
        remote(there, there, og_xs.at[a, k], og_xr.at[a, k], dp=base + k).wait_recv()

    def z_og(a, k):
        there = og_rows(a, base + k, side)
        return remote(there, there, og_zs.at[a, k], og_zr.at[a, k], prec=z_mate)

    def x_act(j):
        return remote(
            act_ref.at[span(y * half, half), pl.ds(j * BLK, BLK)], act_rows(j, me, y),
            act_xs.at[j], act_xr.at[j], dp=over,
        )

    def y_act(j):
        there = act_rows(j, over, y)
        return remote(there, there, act_ys.at[j], act_yr.at[j], pair=y_mate)

    def f_act(j, k):
        there = act_rows(j, over, y if k == 0 else y_mate)
        return remote(there, there, act_fs.at[j, k], act_fr.at[j, k], dp=mate)

    barrier = pltpu.get_barrier_semaphore()
    for device in (dict(dp=mate), dict(dp=base), dict(dp=base + 1), dict(prec=z_mate), dict(pair=y_mate)):
        pl.semaphore_signal(barrier, inc=1, device_id=device, device_id_type=pl.DeviceIdType.MESH)
    pl.semaphore_wait(barrier, 5)

    def send_x(a):
        x_og(a, 0).start()
        x_og(a, 1).start()

    def pass_on_og(a):
        for k in range(2):
            x_og_arrived(a, k)
            z_og(a, k).start()

    def pass_on_act(j):
        x_act(j).wait_recv()
        y_act(j).start()
        f_act(j, 0).start()

    def pass_on_act_again(j):
        y_act(j).wait_recv()
        f_act(j, 1).start()

    def send_local(a, j):
        if j < features:
            core_act(j).start()
            own_act(j).start()
        if a < chunks:
            core_og(a).start()
            own_og(a).start()

    x_act(0).start()
    x_og(0, 0).start()
    send_local(0, 0)
    x_act(0).wait_send()
    x_og(0, 1).start()
    pass_on_act(0)
    x_og(0, 0).wait_send()
    if features > 1:
        x_act(1).start()
    x_og_arrived(0, 0)
    z_og(0, 0).start()
    pass_on_act_again(0)
    x_og(0, 1).wait_send()
    if chunks > 1:
        x_og(1, 0).start()
    x_og_arrived(0, 1)
    z_og(0, 1).start()
    for n in range(1, max(chunks, features)):
        send_local(n, n)
    for j in range(1, features):
        x_act(j).wait_send()
        if j + 1 < features:
            x_act(j + 1).start()
    if chunks > 1:
        x_og(1, 1).start()
    for j in range(1, features):
        pass_on_act(j)
        pass_on_act_again(j)

    def step(a, carry):
        @pl.when((a > 0) & (a + 1 < chunks))
        def _():
            pass_on_og(a + 1)

        @pl.when((a > 0) & (a + 2 < chunks))
        def _():
            send_x(a + 2)

        @pl.when(a == 0)
        def _():
            for j in range(features):
                own_act(j).wait()
                core_act(j).wait_recv()
                f_act(j, 0).wait_recv()
                f_act(j, 1).wait_recv()

        own_og(a).wait()
        core_og(a).wait_recv()
        z_og(a, 0).wait_recv()
        z_og(a, 1).wait_recv()

        both = jnp.concatenate([act_all[j] for j in range(features)], axis=1)
        gradient = dot(og_all[a], both, TN)
        traces, scalings = [], []
        for j in range(features):
            g = gradient[:, j * BLK:(j + 1) * BLK]
            update_ref[a * features + j] = g
            gs = halves(g)
            g_parts[j, 0], g_parts[j, 1] = gs
            left = product(gs, gs, NT)
            left_ref[a * features + j] = left
            l_parts[j, 0], l_parts[j, 1] = halves(left)
            traces.append(total(g * g))
            scalings.append(scaling_of(left, traces[j]))

        @pl.when((a == 0) & (chunks > 1))
        def _():
            pass_on_og(1)

        @pl.when((a == 0) & (chunks > 2))
        def _():
            send_x(2)

        lefts = [(l_parts[j, 0], l_parts[j, 1]) for j in range(features)]
        once = [product(lefts[j], (g_parts[j, 0], g_parts[j, 1])) for j in range(features)]
        for j in range(features):
            s = a * features + j
            main, slope = factor_terms(scalings[j])
            half_way = main * update_ref[s] - slope * once[j]
            twice = product(lefts[j], halves(half_way))
            update = (main * half_way - slope * twice) * jnp.sqrt(scalings[j])
            update_ref[s] = update
            stats_ref[s, 0:1, :] = jnp.broadcast_to(traces[j], (1, 128))
            stats_ref[s, 1:2, :] = jnp.broadcast_to(total(update * update), (1, 128))
            stats_ref[s, 2:3, :] = jnp.broadcast_to(scalings[j], (1, 128))
            stats_ref[s, 3:8, :] = jnp.zeros((5, 128), jnp.float32)
        return carry

    lax.fori_loop(0, chunks, step, 0)

    for a in range(chunks):
        core_og(a).wait_send()
        for k in range(2):
            if a > 0:
                x_og(a, k).wait_send()
            z_og(a, k).wait_send()
    for j in range(features):
        core_act(j).wait_send()
        y_act(j).wait_send()
        f_act(j, 0).wait_send()
        f_act(j, 1).wait_send()


def gathered_updates(og, act):
    shard, rows = og.shape[0], og.shape[1] // lax.axis_size("dp")
    tokens, width = shard * lax.axis_size("dp"), act.shape[1]
    chunks, features = rows // BLK, width // BLK
    blocks = chunks * features
    outside = pl.BlockSpec(memory_space=pltpu.HBM)
    one = pltpu.SemaphoreType.DMA((chunks,))
    two = pltpu.SemaphoreType.DMA((chunks, 2))
    act_one = pltpu.SemaphoreType.DMA((features,))
    act_two = pltpu.SemaphoreType.DMA((features, 2))
    return pl.pallas_call(
        gather_kernel,
        in_specs=[outside, outside],
        out_specs=[pl.BlockSpec(memory_space=pltpu.VMEM)] * 3,
        out_shape=[
            pltpu.VMEM((blocks, BLK, BLK), jnp.float32),
            pltpu.VMEM((blocks, BLK, BLK), jnp.float32),
            pltpu.VMEM((blocks, 8, 128), jnp.float32),
        ],
        scratch_shapes=[
            pltpu.VMEM((chunks, tokens, BLK), jnp.bfloat16),
            pltpu.VMEM((features, tokens, BLK), jnp.bfloat16),
            pltpu.VMEM((features, 2, BLK, BLK), jnp.bfloat16),
            pltpu.VMEM((features, 2, BLK, BLK), jnp.bfloat16),
            one, one, one, two, two, two, two,
            act_one, act_one, act_one, act_one, act_one, act_one, act_one, act_two, act_two,
        ],
        compiler_params=pltpu.CompilerParams(
            collective_id=0, has_side_effects=True, vmem_limit_bytes=36 * 2**20
        ),
    )(og, act)


def finish_kernel(counts_ref, stats_ref, left_ref, update_in, update_ref, squares_ref, coupled_ref):
    del update_in
    features = counts_ref.shape[1]
    squares_ref[...] = jnp.zeros_like(squares_ref)

    def step(s, carry):
        a, j = lax.div(s, features), lax.rem(s, features)
        count = counts_ref[a, j]
        squares_ref[0:8, :] += jnp.broadcast_to(stats_ref[s, 0:1, :], (8, 128))

        @pl.when(count <= 1)
        def _():
            squares_ref[8:16, :] += jnp.broadcast_to(stats_ref[s, 1:2, :], (8, 128))

        @pl.when(count > 1)
        def _():
            coupled_ref[...] = stats_ref[s, 2:3, 0:1] * (left_ref[s] + SHIFT * identity())
            later_iterations(count, coupled_ref, update_ref.at[s])
            u = update_ref[s]
            squares_ref[8:16, :] += jnp.broadcast_to(total(u * u), (8, 128))

        return carry

    lax.fori_loop(0, counts_ref.shape[0] * features, step, 0)


def finished_updates(counts, stats, left, updates):
    vmem = pl.BlockSpec(memory_space=pltpu.VMEM)
    return pl.pallas_call(
        finish_kernel,
        in_specs=[pl.BlockSpec(memory_space=pltpu.SMEM), vmem, vmem, vmem],
        out_specs=[vmem, vmem],
        out_shape=[
            pltpu.VMEM(updates.shape, jnp.float32),
            pltpu.VMEM((16, 128), jnp.float32),
        ],
        scratch_shapes=[pltpu.VMEM((BLK, BLK), jnp.float32)],
        input_output_aliases={3: 0},
        compiler_params=pltpu.CompilerParams(vmem_limit_bytes=36 * 2**20),
    )(counts, stats, left, updates)


def ratio_kernel(groups, squares_ref, ratio_ref, *scratch):
    count = len(groups)
    buffers, sends, recvs = scratch[:count], scratch[count:2 * count], scratch[2 * count:]

    def place(group):
        index = 0
        for name, size in group:
            index = index * size + lax.axis_index(name)
        return index

    def device(group, index):
        found = {}
        for name, size in reversed(group):
            found[name] = lax.rem(index, size)
            index = lax.div(index, size)
        return found

    barrier = pltpu.get_barrier_semaphore()
    partners = 0
    for group in groups:
        extent = math.prod(size for _, size in group)
        for step in range(1, extent):
            pl.semaphore_signal(
                barrier, inc=1, device_id=device(group, lax.rem(place(group) + step, extent)),
                device_id_type=pl.DeviceIdType.MESH,
            )
            partners += 1
    pl.semaphore_wait(barrier, partners)
    sums = squares_ref[...]
    for group, buffer, send, recv in zip(groups, buffers, sends, recvs):
        me, extent = place(group), buffer.shape[0]
        buffer[me] = sums
        copies = []
        for step in range(1, extent):
            copy = remote(
                buffer.at[me], buffer.at[me], send.at[step - 1], recv.at[step - 1],
                **device(group, lax.rem(me + step, extent)),
            )
            copy.start()
            copies.append(copy)
        for copy in copies:
            copy.wait()
        sums = buffer[0]
        for i in range(1, extent):
            sums = sums + buffer[i]
    ratio_ref[...] = jnp.sqrt(sums[0:8, :] / sums[8:16, :])


def graft_ratio(squares):
    sizes = {name: lax.axis_size(name) for name in ("dp", "prec", "pair")}
    groups = [[("dp", sizes["dp"])], [("prec", sizes["prec"]), ("pair", sizes["pair"])]]
    extents = [math.prod(size for _, size in group) for group in groups]
    vmem = pl.BlockSpec(memory_space=pltpu.VMEM)
    sems = [pltpu.SemaphoreType.DMA((max(extent - 1, 1),)) for extent in extents]
    return pl.pallas_call(
        functools.partial(ratio_kernel, groups),
        in_specs=[vmem],
        out_specs=vmem,
        out_shape=jax.ShapeDtypeStruct((8, 128), jnp.float32),
        scratch_shapes=[pltpu.VMEM((extent, 16, 128), jnp.float32) for extent in extents] + sems + sems,
        compiler_params=pltpu.CompilerParams(
            collective_id=1, has_side_effects=True, vmem_limit_bytes=8 * 2**20
        ),
    )(squares)


def scale_kernel(ratio_ref, update_ref, out_ref):
    out_ref[...] = update_ref[...] * ratio_ref[0:1, 0:1]


def scaled_updates(ratio, updates):
    rows, width = updates.shape
    block = pl.BlockSpec((BLK // 2, width), lambda i: (i, 0))
    return pl.pallas_call(
        scale_kernel,
        grid=(rows // (BLK // 2),),
        in_specs=[pl.BlockSpec(memory_space=pltpu.VMEM), block],
        out_specs=block,
        out_shape=jax.ShapeDtypeStruct(updates.shape, jnp.float32),
        compiler_params=pltpu.CompilerParams(vmem_limit_bytes=48 * 2**20),
    )(ratio, updates)


def scale_blocks_kernel(ratio_ref, update_ref, out_ref, scaled, sem):
    features = out_ref.shape[1] // BLK

    def place(s):
        a, j = lax.div(s, features), lax.rem(s, features)
        there = out_ref.at[
            pl.ds(pl.multiple_of(a * BLK, BLK), BLK), pl.ds(pl.multiple_of(j * BLK, BLK), BLK)
        ]
        return pltpu.make_async_copy(scaled.at[s], there, sem.at[s])

    def scale(s, carry):
        scaled[s] = update_ref[s] * ratio_ref[0:1, 0:1]
        place(s).start()
        return carry

    def wait(s, carry):
        place(s).wait()
        return carry

    lax.fori_loop(0, scaled.shape[0], scale, 0)
    lax.fori_loop(0, scaled.shape[0], wait, 0)


def scaled_blocks(ratio, updates, shape):
    vmem = pl.BlockSpec(memory_space=pltpu.VMEM)
    return pl.pallas_call(
        scale_blocks_kernel,
        in_specs=[vmem, vmem],
        out_specs=pl.BlockSpec(memory_space=pl.ANY),
        out_shape=jax.ShapeDtypeStruct(shape, jnp.float32),
        scratch_shapes=[
            pltpu.VMEM(updates.shape, jnp.float32),
            pltpu.SemaphoreType.DMA((updates.shape[0],)),
        ],
        compiler_params=pltpu.CompilerParams(vmem_limit_bytes=36 * 2**20),
    )(ratio, updates)


def gathered_first(activations, output_grads, iter_counts):
    act = lax.all_gather(activations, "dp", axis=0, tiled=True)
    og = lax.all_to_all(output_grads, "dp", split_axis=1, concat_axis=0, tiled=True)
    return local_updates(og, act, iter_counts)


def per_device(activations, output_grads, iter_counts):
    sizes = [lax.axis_size(name) for name in ("dp", "prec", "pair")]
    if sizes[0] == 4 and sizes[1] % 2 == 0 and sizes[2] == 2:
        updates, left, stats = gathered_updates(output_grads, activations)
        updates, squares = finished_updates(iter_counts, stats, left, updates)
        shape = (output_grads.shape[1] // sizes[0], activations.shape[1])
        return scaled_blocks(graft_ratio(squares), updates, shape)
    updates, squares = gathered_first(activations, output_grads, iter_counts)
    return scaled_updates(graft_ratio(squares), updates)


def solution(mesh):
    in_specs = (P("dp", "prec"), P("dp", "pair"), P(("pair", "dp"), "prec"))
    out_specs = P(("pair", "dp"), "prec")
    return jax.shard_map(
        per_device, mesh=mesh, in_specs=in_specs, out_specs=out_specs, check_vma=False
    )
```

```python
import functools
import math
import jax
import jax.numpy as jnp
from jax import lax
from jax.experimental import pallas as pl
from jax.experimental.pallas import tpu as pltpu
from jax.sharding import PartitionSpec as P

BLK = 512
SHIFT = 0.001
NN = (((1,), (0,)), ((), ()))
NT = (((1,), (1,)), ((), ()))
TN = (((0,), (0,)), ((), ()))


def halves(x):
    high = x.astype(jnp.bfloat16)
    low = (x - high.astype(jnp.float32)).astype(jnp.bfloat16)
    return high, low


def dot(a, b, dims):
    return lax.dot_general(a, b, dims, preferred_element_type=jnp.float32)


def product(a, b, dims=NN):
    depth = dims[0][1][0]
    left = jnp.concatenate([a[0], a[0], a[1]], axis=1)
    return dot(left, jnp.concatenate([b[0], b[1], b[0]], axis=depth), dims)


def symmetric_product(a, b, dims=NN):
    middle = BLK // 2
    upper = product([part[:middle] for part in a], b, dims)
    right = [part[middle:] if dims == NT else part[:, middle:] for part in b]
    corner = product([part[middle:] for part in a], right, dims)
    lower = jnp.concatenate([upper[:, middle:].T, corner], axis=1)
    return jnp.concatenate([upper, lower], axis=0)


def total(x):
    return jnp.sum(x, keepdims=True)


def scaling_of(left, trace):
    norm = total(left * left) + (2.0 * SHIFT) * trace + BLK * SHIFT * SHIFT
    return 2.5 / jnp.sqrt(norm + 1e-06)


def factor_terms(scaling):
    return 1.25 - (0.25 * SHIFT) * scaling, 0.25 * scaling


def first_iteration(g):
    gs = halves(g)
    left = symmetric_product(gs, gs, NT)
    trace = total(g * g)
    scaling = scaling_of(left, trace)
    main, slope = factor_terms(scaling)
    ls = halves(left)
    half = main * g - slope * product(ls, gs)
    update = (main * half - slope * product(ls, halves(half))) * jnp.sqrt(scaling)
    return left, scaling, trace, update


def identity():
    rows = lax.broadcasted_iota(jnp.int32, (BLK, BLK), 0)
    return (rows == lax.broadcasted_iota(jnp.int32, (BLK, BLK), 1)).astype(jnp.float32)


def later_iterations(count, coupled_ref, update_ref):
    def advance(_, carry):
        coupled = coupled_ref[...]
        factor = halves(1.25 * identity() - 0.25 * coupled)
        square = halves(symmetric_product(factor, factor))
        fourth = halves(symmetric_product(square, square))
        coupled = symmetric_product(fourth, halves(coupled))
        coupled_ref[...] = coupled
        factor = halves(1.25 * identity() - 0.25 * coupled)
        once = product(factor, halves(update_ref[...]))
        update_ref[...] = product(factor, halves(once))
        return carry

    lax.fori_loop(1, count, advance, 0)


def block_kernel(counts_ref, og_ref, act_ref, update_ref, squares_ref, coupled_ref):
    i, j = pl.program_id(0), pl.program_id(1)

    @pl.when((i == 0) & (j == 0))
    def _():
        squares_ref[...] = jnp.zeros_like(squares_ref)

    g = dot(og_ref[...], act_ref[...], TN)
    left, scaling, trace, update = first_iteration(g)
    update_ref[...] = update
    count = counts_ref[i, j]

    @pl.when(count > 1)
    def _():
        coupled_ref[...] = scaling * (left + SHIFT * identity())
        later_iterations(count, coupled_ref, update_ref)

    u = update_ref[...]
    squares_ref[0:8, :] += jnp.broadcast_to(trace, (8, 128))
    squares_ref[8:16, :] += jnp.broadcast_to(total(u * u), (8, 128))


def local_updates(og, act, counts):
    tokens, rows = og.shape
    features = act.shape[1]
    grid = (rows // BLK, features // BLK)
    return pl.pallas_call(
        block_kernel,
        grid=grid,
        in_specs=[
            pl.BlockSpec(memory_space=pltpu.SMEM),
            pl.BlockSpec((tokens, BLK), lambda i, j: (0, i)),
            pl.BlockSpec((tokens, BLK), lambda i, j: (0, j)),
        ],
        out_specs=[
            pl.BlockSpec((BLK, BLK), lambda i, j: (i, j)),
            pl.BlockSpec((16, 128), lambda i, j: (0, 0)),
        ],
        out_shape=[
            jax.ShapeDtypeStruct((rows, features), jnp.float32),
            jax.ShapeDtypeStruct((16, 128), jnp.float32),
        ],
        scratch_shapes=[pltpu.VMEM((BLK, BLK), jnp.float32)],
        compiler_params=pltpu.CompilerParams(vmem_limit_bytes=48 * 2**20),
    )(counts, og, act)


def remote(src, dst, send, recv, **device):
    return pltpu.make_async_remote_copy(
        src_ref=src, dst_ref=dst, send_sem=send, recv_sem=recv,
        device_id=device, device_id_type=pl.DeviceIdType.MESH,
    )


def gather_kernel(
    og_ref, act_ref, update_ref, left_ref, stats_ref,
    og_all, act_all, g_parts, l_parts,
    og_own, og_cs, og_cr, og_xs, og_xr, og_zs, og_zr,
    act_own, act_cs, act_cr, act_xs, act_xr, act_ys, act_yr, act_fs, act_fr,
):
    shard = og_ref.shape[0]
    half = shard // 2
    chunks, features = og_all.shape[0], act_all.shape[0]
    width = chunks * BLK
    me, z, y = lax.axis_index("dp"), lax.axis_index("prec"), lax.axis_index("pair")
    x, core = lax.div(me, 2), lax.rem(me, 2)
    mate, over, base = me + 1 - 2 * core, me + 2 - 4 * x, 2 - 2 * x
    over_mate = base + 1 - core
    side = lax.rem(z, 2)
    z_mate, y_mate = z + 1 - 2 * side, 1 - y

    def span(start, size):
        return pl.ds(pl.multiple_of(start, 128), size)

    def og_columns(device, a):
        return span(device * width + a * BLK, BLK)

    def og_rows(a, device, part):
        return og_all.at[a, span(device * shard + part * half, half)]

    def act_rows(j, device, part):
        return act_all.at[j, span(device * shard + part * half, half)]

    def own_og(a):
        return pltpu.make_async_copy(
            og_ref.at[:, og_columns(me, a)], og_all.at[a, span(me * shard, shard)], og_own.at[a]
        )

    def own_act(j):
        return pltpu.make_async_copy(
            act_ref.at[:, span(j * BLK, BLK)], act_all.at[j, span(me * shard, shard)], act_own.at[j]
        )

    def core_og(a):
        return remote(
            og_ref.at[:, og_columns(mate, a)], og_all.at[a, span(me * shard, shard)],
            og_cs.at[a], og_cr.at[a], dp=mate,
        )

    def core_act(j):
        return remote(
            act_ref.at[:, span(j * BLK, BLK)], act_all.at[j, span(me * shard, shard)],
            act_cs.at[j], act_cr.at[j], dp=mate,
        )

    def x_og(a, k):
        return remote(
            og_ref.at[span(side * half, half), og_columns(base + k, a)], og_rows(a, me, side),
            og_xs.at[a, k], og_xr.at[a, core], dp=base + k,
        )

    def x_og_arrived(a, k):
        there = og_rows(a, base + k, side)
        remote(there, there, og_xs.at[a, k], og_xr.at[a, k], dp=base + k).wait_recv()

    def z_og(a, k):
        there = og_rows(a, base + k, side)
        return remote(there, there, og_zs.at[a, k], og_zr.at[a, k], prec=z_mate)

    def x_act(j):
        return remote(
            act_ref.at[span(y * half, half), pl.ds(j * BLK, BLK)], act_rows(j, me, y),
            act_xs.at[j], act_xr.at[j], dp=over,
        )

    def y_act(j):
        there = act_rows(j, over, y)
        return remote(there, there, act_ys.at[j], act_yr.at[j], pair=y_mate)

    def f_act(j, k):
        there = act_rows(j, over, y if k == 0 else y_mate)
        return remote(there, there, act_fs.at[j, k], act_fr.at[j, k], dp=mate)

    barrier = pltpu.get_barrier_semaphore()
    for device in (dict(dp=mate), dict(dp=base), dict(dp=base + 1), dict(prec=z_mate), dict(pair=y_mate)):
        pl.semaphore_signal(barrier, inc=1, device_id=device, device_id_type=pl.DeviceIdType.MESH)
    pl.semaphore_wait(barrier, 5)

    def send_x(a):
        x_og(a, 0).start()
        x_og(a, 1).start()

    def pass_on_og(a):
        for k in range(2):
            x_og_arrived(a, k)
            z_og(a, k).start()

    def pass_on_act(j):
        x_act(j).wait_recv()
        y_act(j).start()
        f_act(j, 0).start()

    def pass_on_act_again(j):
        y_act(j).wait_recv()
        f_act(j, 1).start()

    def send_local(a, j):
        if j < features:
            core_act(j).start()
            own_act(j).start()
        if a < chunks:
            core_og(a).start()
            own_og(a).start()

    x_act(0).start()
    x_og(0, 0).start()
    send_local(0, 0)
    x_act(0).wait_send()
    x_og(0, 1).start()
    pass_on_act(0)
    x_og(0, 0).wait_send()
    if features > 1:
        x_act(1).start()
    x_og_arrived(0, 0)
    z_og(0, 0).start()
    pass_on_act_again(0)
    x_og(0, 1).wait_send()
    if chunks > 1:
        x_og(1, 0).start()
    x_og_arrived(0, 1)
    z_og(0, 1).start()
    for n in range(1, max(chunks, features)):
        send_local(n, n)
    for j in range(1, features):
        x_act(j).wait_send()
        if j + 1 < features:
            x_act(j + 1).start()
    if chunks > 1:
        x_og(1, 1).start()
    for j in range(1, features):
        pass_on_act(j)
        pass_on_act_again(j)
    if chunks > 2:
        send_x(2)

    def step(a, carry):
        @pl.when((a > 0) & (a + 1 < chunks))
        def _():
            pass_on_og(a + 1)

        @pl.when((a > 0) & (a + 3 < chunks))
        def _():
            send_x(a + 3)

        @pl.when(a == 0)
        def _():
            for j in range(features):
                own_act(j).wait()
                core_act(j).wait_recv()
                f_act(j, 0).wait_recv()
                f_act(j, 1).wait_recv()

        own_og(a).wait()
        core_og(a).wait_recv()
        z_og(a, 0).wait_recv()
        z_og(a, 1).wait_recv()

        both = jnp.concatenate([act_all[j] for j in range(features)], axis=1)
        gradient = dot(og_all[a], both, TN)
        traces, scalings = [], []
        for j in range(features):
            g = gradient[:, j * BLK:(j + 1) * BLK]
            update_ref[a * features + j] = g
            gs = halves(g)
            g_parts[j, 0], g_parts[j, 1] = gs
            left = symmetric_product(gs, gs, NT)
            left_ref[a * features + j] = left
            l_parts[j, 0], l_parts[j, 1] = halves(left)
            traces.append(total(g * g))
            scalings.append(scaling_of(left, traces[j]))

        @pl.when((a == 0) & (chunks > 1))
        def _():
            pass_on_og(1)

        @pl.when((a == 0) & (chunks > 3))
        def _():
            send_x(3)

        lefts = [(l_parts[j, 0], l_parts[j, 1]) for j in range(features)]
        once = [product(lefts[j], (g_parts[j, 0], g_parts[j, 1])) for j in range(features)]
        for j in range(features):
            s = a * features + j
            main, slope = factor_terms(scalings[j])
            half_way = main * update_ref[s] - slope * once[j]
            twice = product(lefts[j], halves(half_way))
            update = (main * half_way - slope * twice) * jnp.sqrt(scalings[j])
            update_ref[s] = update
            stats_ref[s, 0:1, :] = jnp.broadcast_to(traces[j], (1, 128))
            stats_ref[s, 1:2, :] = jnp.broadcast_to(total(update * update), (1, 128))
            stats_ref[s, 2:3, :] = jnp.broadcast_to(scalings[j], (1, 128))
            stats_ref[s, 3:8, :] = jnp.zeros((5, 128), jnp.float32)
        return carry

    lax.fori_loop(0, chunks, step, 0)

    for a in range(chunks):
        core_og(a).wait_send()
        for k in range(2):
            if a > 0:
                x_og(a, k).wait_send()
            z_og(a, k).wait_send()
    for j in range(features):
        core_act(j).wait_send()
        y_act(j).wait_send()
        f_act(j, 0).wait_send()
        f_act(j, 1).wait_send()


def gathered_updates(og, act):
    shard, rows = og.shape[0], og.shape[1] // lax.axis_size("dp")
    tokens, width = shard * lax.axis_size("dp"), act.shape[1]
    chunks, features = rows // BLK, width // BLK
    blocks = chunks * features
    outside = pl.BlockSpec(memory_space=pltpu.HBM)
    one = pltpu.SemaphoreType.DMA((chunks,))
    two = pltpu.SemaphoreType.DMA((chunks, 2))
    act_one = pltpu.SemaphoreType.DMA((features,))
    act_two = pltpu.SemaphoreType.DMA((features, 2))
    return pl.pallas_call(
        gather_kernel,
        in_specs=[outside, outside],
        out_specs=[pl.BlockSpec(memory_space=pltpu.VMEM)] * 3,
        out_shape=[
            pltpu.VMEM((blocks, BLK, BLK), jnp.float32),
            pltpu.VMEM((blocks, BLK, BLK), jnp.float32),
            pltpu.VMEM((blocks, 8, 128), jnp.float32),
        ],
        scratch_shapes=[
            pltpu.VMEM((chunks, tokens, BLK), jnp.bfloat16),
            pltpu.VMEM((features, tokens, BLK), jnp.bfloat16),
            pltpu.VMEM((features, 2, BLK, BLK), jnp.bfloat16),
            pltpu.VMEM((features, 2, BLK, BLK), jnp.bfloat16),
            one, one, one, two, two, two, two,
            act_one, act_one, act_one, act_one, act_one, act_one, act_one, act_two, act_two,
        ],
        compiler_params=pltpu.CompilerParams(
            collective_id=0, has_side_effects=True, vmem_limit_bytes=36 * 2**20
        ),
    )(og, act)


def finish_kernel(counts_ref, stats_ref, left_ref, update_in, update_ref, squares_ref, coupled_ref):
    del update_in
    features = counts_ref.shape[1]
    squares_ref[...] = jnp.zeros_like(squares_ref)

    def step(s, carry):
        a, j = lax.div(s, features), lax.rem(s, features)
        count = counts_ref[a, j]
        squares_ref[0:8, :] += jnp.broadcast_to(stats_ref[s, 0:1, :], (8, 128))

        @pl.when(count <= 1)
        def _():
            squares_ref[8:16, :] += jnp.broadcast_to(stats_ref[s, 1:2, :], (8, 128))

        @pl.when(count > 1)
        def _():
            coupled_ref[...] = stats_ref[s, 2:3, 0:1] * (left_ref[s] + SHIFT * identity())
            later_iterations(count, coupled_ref, update_ref.at[s])
            u = update_ref[s]
            squares_ref[8:16, :] += jnp.broadcast_to(total(u * u), (8, 128))

        return carry

    lax.fori_loop(0, counts_ref.shape[0] * features, step, 0)


def finished_updates(counts, stats, left, updates):
    vmem = pl.BlockSpec(memory_space=pltpu.VMEM)
    return pl.pallas_call(
        finish_kernel,
        in_specs=[pl.BlockSpec(memory_space=pltpu.SMEM), vmem, vmem, vmem],
        out_specs=[vmem, vmem],
        out_shape=[
            pltpu.VMEM(updates.shape, jnp.float32),
            pltpu.VMEM((16, 128), jnp.float32),
        ],
        scratch_shapes=[pltpu.VMEM((BLK, BLK), jnp.float32)],
        input_output_aliases={3: 0},
        compiler_params=pltpu.CompilerParams(vmem_limit_bytes=36 * 2**20),
    )(counts, stats, left, updates)


def ratio_kernel(groups, squares_ref, ratio_ref, *scratch):
    count = len(groups)
    buffers, sends, recvs = scratch[:count], scratch[count:2 * count], scratch[2 * count:]

    def place(group):
        index = 0
        for name, size in group:
            index = index * size + lax.axis_index(name)
        return index

    def device(group, index):
        found = {}
        for name, size in reversed(group):
            found[name] = lax.rem(index, size)
            index = lax.div(index, size)
        return found

    barrier = pltpu.get_barrier_semaphore()
    partners = 0
    for group in groups:
        extent = math.prod(size for _, size in group)
        for step in range(1, extent):
            pl.semaphore_signal(
                barrier, inc=1, device_id=device(group, lax.rem(place(group) + step, extent)),
                device_id_type=pl.DeviceIdType.MESH,
            )
            partners += 1
    pl.semaphore_wait(barrier, partners)
    sums = squares_ref[...]
    for group, buffer, send, recv in zip(groups, buffers, sends, recvs):
        me, extent = place(group), buffer.shape[0]
        buffer[me] = sums
        copies = []
        for step in range(1, extent):
            copy = remote(
                buffer.at[me], buffer.at[me], send.at[step - 1], recv.at[step - 1],
                **device(group, lax.rem(me + step, extent)),
            )
            copy.start()
            copies.append(copy)
        for copy in copies:
            copy.wait()
        sums = buffer[0]
        for i in range(1, extent):
            sums = sums + buffer[i]
    ratio_ref[...] = jnp.sqrt(sums[0:8, :] / sums[8:16, :])


def graft_ratio(squares):
    sizes = {name: lax.axis_size(name) for name in ("dp", "prec", "pair")}
    groups = [[("dp", sizes["dp"])], [("prec", sizes["prec"]), ("pair", sizes["pair"])]]
    extents = [math.prod(size for _, size in group) for group in groups]
    vmem = pl.BlockSpec(memory_space=pltpu.VMEM)
    sems = [pltpu.SemaphoreType.DMA((max(extent - 1, 1),)) for extent in extents]
    return pl.pallas_call(
        functools.partial(ratio_kernel, groups),
        in_specs=[vmem],
        out_specs=vmem,
        out_shape=jax.ShapeDtypeStruct((8, 128), jnp.float32),
        scratch_shapes=[pltpu.VMEM((extent, 16, 128), jnp.float32) for extent in extents] + sems + sems,
        compiler_params=pltpu.CompilerParams(
            collective_id=1, has_side_effects=True, vmem_limit_bytes=8 * 2**20
        ),
    )(squares)


def scale_kernel(ratio_ref, update_ref, out_ref):
    out_ref[...] = update_ref[...] * ratio_ref[0:1, 0:1]


def scaled_updates(ratio, updates):
    rows, width = updates.shape
    block = pl.BlockSpec((BLK // 2, width), lambda i: (i, 0))
    return pl.pallas_call(
        scale_kernel,
        grid=(rows // (BLK // 2),),
        in_specs=[pl.BlockSpec(memory_space=pltpu.VMEM), block],
        out_specs=block,
        out_shape=jax.ShapeDtypeStruct(updates.shape, jnp.float32),
        compiler_params=pltpu.CompilerParams(vmem_limit_bytes=48 * 2**20),
    )(ratio, updates)


def scale_blocks_kernel(ratio_ref, update_ref, out_ref, scaled, sem):
    features = out_ref.shape[1] // BLK

    def place(s):
        a, j = lax.div(s, features), lax.rem(s, features)
        there = out_ref.at[
            pl.ds(pl.multiple_of(a * BLK, BLK), BLK), pl.ds(pl.multiple_of(j * BLK, BLK), BLK)
        ]
        return pltpu.make_async_copy(scaled.at[s], there, sem.at[s])

    def scale(s, carry):
        scaled[s] = update_ref[s] * ratio_ref[0:1, 0:1]
        place(s).start()
        return carry

    def wait(s, carry):
        place(s).wait()
        return carry

    lax.fori_loop(0, scaled.shape[0], scale, 0)
    lax.fori_loop(0, scaled.shape[0], wait, 0)


def scaled_blocks(ratio, updates, shape):
    vmem = pl.BlockSpec(memory_space=pltpu.VMEM)
    return pl.pallas_call(
        scale_blocks_kernel,
        in_specs=[vmem, vmem],
        out_specs=pl.BlockSpec(memory_space=pl.ANY),
        out_shape=jax.ShapeDtypeStruct(shape, jnp.float32),
        scratch_shapes=[
            pltpu.VMEM(updates.shape, jnp.float32),
            pltpu.SemaphoreType.DMA((updates.shape[0],)),
        ],
        compiler_params=pltpu.CompilerParams(vmem_limit_bytes=36 * 2**20),
    )(ratio, updates)


def gathered_first(activations, output_grads, iter_counts):
    act = lax.all_gather(activations, "dp", axis=0, tiled=True)
    og = lax.all_to_all(output_grads, "dp", split_axis=1, concat_axis=0, tiled=True)
    return local_updates(og, act, iter_counts)


def per_device(activations, output_grads, iter_counts):
    sizes = [lax.axis_size(name) for name in ("dp", "prec", "pair")]
    if sizes[0] == 4 and sizes[1] % 2 == 0 and sizes[2] == 2:
        updates, left, stats = gathered_updates(output_grads, activations)
        updates, squares = finished_updates(iter_counts, stats, left, updates)
        shape = (output_grads.shape[1] // sizes[0], activations.shape[1])
        return scaled_blocks(graft_ratio(squares), updates, shape)
    updates, squares = gathered_first(activations, output_grads, iter_counts)
    return scaled_updates(graft_ratio(squares), updates)


def solution(mesh):
    in_specs = (P("dp", "prec"), P("dp", "pair"), P(("pair", "dp"), "prec"))
    out_specs = P(("pair", "dp"), "prec")
    return jax.shard_map(
        per_device, mesh=mesh, in_specs=in_specs, out_specs=out_specs, check_vma=False
    )
```

```python
import functools
import math
import jax
import jax.numpy as jnp
from jax import lax
from jax.experimental import pallas as pl
from jax.experimental.pallas import tpu as pltpu
from jax.sharding import PartitionSpec as P

BLK = 512
SHIFT = 0.001
NN = (((1,), (0,)), ((), ()))
NT = (((1,), (1,)), ((), ()))
TN = (((0,), (0,)), ((), ()))


def halves(x):
    high = x.astype(jnp.bfloat16)
    low = (x - high.astype(jnp.float32)).astype(jnp.bfloat16)
    return high, low


def dot(a, b, dims):
    return lax.dot_general(a, b, dims, preferred_element_type=jnp.float32)


def product(a, b, dims=NN):
    depth = dims[0][1][0]
    left = jnp.concatenate([a[0], a[0], a[1]], axis=1)
    return dot(left, jnp.concatenate([b[0], b[1], b[0]], axis=depth), dims)


def symmetric_product(a, b, dims=NN):
    middle = BLK // 2
    upper = product([part[:middle] for part in a], b, dims)
    right = [part[middle:] if dims == NT else part[:, middle:] for part in b]
    corner = product([part[middle:] for part in a], right, dims)
    lower = jnp.concatenate([upper[:, middle:].T, corner], axis=1)
    return jnp.concatenate([upper, lower], axis=0)


def total(x):
    return jnp.sum(x, keepdims=True)


def scaling_of(left, trace):
    norm = total(left * left) + (2.0 * SHIFT) * trace + BLK * SHIFT * SHIFT
    return 2.5 / jnp.sqrt(norm + 1e-06)


def factor_terms(scaling):
    return 1.25 - (0.25 * SHIFT) * scaling, 0.25 * scaling


def first_iteration(g):
    gs = halves(g)
    left = symmetric_product(gs, gs, NT)
    trace = total(g * g)
    scaling = scaling_of(left, trace)
    main, slope = factor_terms(scaling)
    ls = halves(left)
    half = main * g - slope * product(ls, gs)
    update = (main * half - slope * product(ls, halves(half))) * jnp.sqrt(scaling)
    return left, scaling, trace, update


def identity():
    rows = lax.broadcasted_iota(jnp.int32, (BLK, BLK), 0)
    return (rows == lax.broadcasted_iota(jnp.int32, (BLK, BLK), 1)).astype(jnp.float32)


def later_iterations(count, coupled_ref, update_ref):
    def advance(_, carry):
        coupled = coupled_ref[...]
        factor = halves(1.25 * identity() - 0.25 * coupled)
        square = halves(symmetric_product(factor, factor))
        fourth = halves(symmetric_product(square, square))
        coupled = symmetric_product(fourth, halves(coupled))
        coupled_ref[...] = coupled
        factor = halves(1.25 * identity() - 0.25 * coupled)
        once = product(factor, halves(update_ref[...]))
        update_ref[...] = product(factor, halves(once))
        return carry

    lax.fori_loop(1, count, advance, 0)


def block_kernel(counts_ref, og_ref, act_ref, update_ref, squares_ref, coupled_ref):
    i, j = pl.program_id(0), pl.program_id(1)

    @pl.when((i == 0) & (j == 0))
    def _():
        squares_ref[...] = jnp.zeros_like(squares_ref)

    g = dot(og_ref[...], act_ref[...], TN)
    left, scaling, trace, update = first_iteration(g)
    update_ref[...] = update
    count = counts_ref[i, j]

    @pl.when(count > 1)
    def _():
        coupled_ref[...] = scaling * (left + SHIFT * identity())
        later_iterations(count, coupled_ref, update_ref)

    u = update_ref[...]
    squares_ref[0:8, :] += jnp.broadcast_to(trace, (8, 128))
    squares_ref[8:16, :] += jnp.broadcast_to(total(u * u), (8, 128))


def local_updates(og, act, counts):
    tokens, rows = og.shape
    features = act.shape[1]
    grid = (rows // BLK, features // BLK)
    return pl.pallas_call(
        block_kernel,
        grid=grid,
        in_specs=[
            pl.BlockSpec(memory_space=pltpu.SMEM),
            pl.BlockSpec((tokens, BLK), lambda i, j: (0, i)),
            pl.BlockSpec((tokens, BLK), lambda i, j: (0, j)),
        ],
        out_specs=[
            pl.BlockSpec((BLK, BLK), lambda i, j: (i, j)),
            pl.BlockSpec((16, 128), lambda i, j: (0, 0)),
        ],
        out_shape=[
            jax.ShapeDtypeStruct((rows, features), jnp.float32),
            jax.ShapeDtypeStruct((16, 128), jnp.float32),
        ],
        scratch_shapes=[pltpu.VMEM((BLK, BLK), jnp.float32)],
        compiler_params=pltpu.CompilerParams(vmem_limit_bytes=48 * 2**20),
    )(counts, og, act)


def remote(src, dst, send, recv, **device):
    return pltpu.make_async_remote_copy(
        src_ref=src, dst_ref=dst, send_sem=send, recv_sem=recv,
        device_id=device, device_id_type=pl.DeviceIdType.MESH,
    )


def gather_kernel(
    og_ref, act_ref, update_ref, left_ref, stats_ref,
    og_all, act_all, g_parts, l_parts,
    og_own, og_cs, og_cr, og_xs, og_xr, og_zs, og_zr,
    act_own, act_cs, act_cr, act_xs, act_xr, act_ys, act_yr, act_fs, act_fr,
):
    shard = og_ref.shape[0]
    half = shard // 2
    chunks, features = og_all.shape[0], act_all.shape[0]
    width = chunks * BLK
    me, z, y = lax.axis_index("dp"), lax.axis_index("prec"), lax.axis_index("pair")
    x, core = lax.div(me, 2), lax.rem(me, 2)
    mate, over, base = me + 1 - 2 * core, me + 2 - 4 * x, 2 - 2 * x
    over_mate = base + 1 - core
    side = lax.rem(z, 2)
    z_mate, y_mate = z + 1 - 2 * side, 1 - y

    def span(start, size):
        return pl.ds(pl.multiple_of(start, 128), size)

    def og_columns(device, a):
        return span(device * width + a * BLK, BLK)

    def og_rows(a, device, part):
        return og_all.at[a, span(device * shard + part * half, half)]

    def act_rows(j, device, part):
        return act_all.at[j, span(device * shard + part * half, half)]

    def own_og(a):
        return pltpu.make_async_copy(
            og_ref.at[:, og_columns(me, a)], og_all.at[a, span(me * shard, shard)], og_own.at[a]
        )

    def own_act(j):
        return pltpu.make_async_copy(
            act_ref.at[:, span(j * BLK, BLK)], act_all.at[j, span(me * shard, shard)], act_own.at[j]
        )

    def core_og(a):
        return remote(
            og_ref.at[:, og_columns(mate, a)], og_all.at[a, span(me * shard, shard)],
            og_cs.at[a], og_cr.at[a], dp=mate,
        )

    def core_act(j):
        return remote(
            act_ref.at[:, span(j * BLK, BLK)], act_all.at[j, span(me * shard, shard)],
            act_cs.at[j], act_cr.at[j], dp=mate,
        )

    def x_og(a, k):
        return remote(
            og_ref.at[span(side * half, half), og_columns(base + k, a)], og_rows(a, me, side),
            og_xs.at[a, k], og_xr.at[a, core], dp=base + k,
        )

    def x_og_arrived(a, k):
        there = og_rows(a, base + k, side)
        remote(there, there, og_xs.at[a, k], og_xr.at[a, k], dp=base + k).wait_recv()

    def z_og(a, k):
        there = og_rows(a, base + k, side)
        return remote(there, there, og_zs.at[a, k], og_zr.at[a, k], prec=z_mate)

    def x_act(j):
        return remote(
            act_ref.at[span(y * half, half), pl.ds(j * BLK, BLK)], act_rows(j, me, y),
            act_xs.at[j], act_xr.at[j], dp=over,
        )

    def y_act(j):
        there = act_rows(j, over, y)
        return remote(there, there, act_ys.at[j], act_yr.at[j], pair=y_mate)

    def f_act(j, k):
        there = act_rows(j, over, y if k == 0 else y_mate)
        return remote(there, there, act_fs.at[j, k], act_fr.at[j, k], dp=mate)

    barrier = pltpu.get_barrier_semaphore()
    for device in (dict(dp=mate), dict(dp=base), dict(dp=base + 1), dict(prec=z_mate), dict(pair=y_mate)):
        pl.semaphore_signal(barrier, inc=1, device_id=device, device_id_type=pl.DeviceIdType.MESH)
    pl.semaphore_wait(barrier, 5)

    def send_x(a):
        x_og(a, 0).start()
        x_og(a, 1).start()

    def pass_on_og(a):
        for k in range(2):
            x_og_arrived(a, k)
            z_og(a, k).start()

    def pass_on_act(j):
        x_act(j).wait_recv()
        y_act(j).start()
        f_act(j, 0).start()

    def pass_on_act_again(j):
        y_act(j).wait_recv()
        f_act(j, 1).start()

    def send_local(a, j):
        if j < features:
            core_act(j).start()
            own_act(j).start()
        if a < chunks:
            core_og(a).start()
            own_og(a).start()

    def gradient_of(a, x_side):
        rows = span(x_side * 2 * shard, 2 * shard)
        both = jnp.concatenate([act_all[j, rows] for j in range(features)], axis=1)
        return dot(og_all[a, rows], both, TN)

    def near_gradient(a):
        if a < chunks:
            own_og(a).wait()
            core_og(a).wait_recv()
            gradient = gradient_of(a, x)
            for j in range(features):
                update_ref[a * features + j] = gradient[:, j * BLK:(j + 1) * BLK]

    x_act(0).start()
    x_og(0, 0).start()
    for n in range(max(chunks, features)):
        send_local(n, n)
    x_act(0).wait_send()
    x_og(0, 1).start()
    pass_on_act(0)
    x_og(0, 0).wait_send()
    if features > 1:
        x_act(1).start()
    x_og_arrived(0, 0)
    z_og(0, 0).start()
    for j in range(features):
        own_act(j).wait()
        core_act(j).wait_recv()
    near_gradient(0)
    pass_on_act_again(0)
    x_og(0, 1).wait_send()
    if chunks > 1:
        x_og(1, 0).start()
    x_og_arrived(0, 1)
    z_og(0, 1).start()
    for j in range(1, features):
        x_act(j).wait_send()
        if j + 1 < features:
            x_act(j + 1).start()
    if chunks > 1:
        x_og(1, 1).start()
    for j in range(1, features):
        pass_on_act(j)
    near_gradient(1)
    near_gradient(2)
    for j in range(1, features):
        pass_on_act_again(j)
    if chunks > 2:
        send_x(2)
    for a in range(3, chunks):
        near_gradient(a)

    def step(a, carry):
        @pl.when((a > 0) & (a + 1 < chunks))
        def _():
            pass_on_og(a + 1)

        @pl.when((a > 0) & (a + 3 < chunks))
        def _():
            send_x(a + 3)

        @pl.when(a == 0)
        def _():
            for j in range(features):
                f_act(j, 0).wait_recv()
                f_act(j, 1).wait_recv()

        z_og(a, 0).wait_recv()
        z_og(a, 1).wait_recv()

        gradient = gradient_of(a, 1 - x)
        traces, scalings = [], []
        for j in range(features):
            g = update_ref[a * features + j] + gradient[:, j * BLK:(j + 1) * BLK]
            update_ref[a * features + j] = g
            gs = halves(g)
            g_parts[j, 0], g_parts[j, 1] = gs
            left = symmetric_product(gs, gs, NT)
            left_ref[a * features + j] = left
            l_parts[j, 0], l_parts[j, 1] = halves(left)
            traces.append(total(g * g))
            scalings.append(scaling_of(left, traces[j]))

        @pl.when((a == 0) & (chunks > 1))
        def _():
            pass_on_og(1)

        @pl.when((a == 0) & (chunks > 3))
        def _():
            send_x(3)

        lefts = [(l_parts[j, 0], l_parts[j, 1]) for j in range(features)]
        once = [product(lefts[j], (g_parts[j, 0], g_parts[j, 1])) for j in range(features)]
        for j in range(features):
            s = a * features + j
            main, slope = factor_terms(scalings[j])
            half_way = main * update_ref[s] - slope * once[j]
            twice = product(lefts[j], halves(half_way))
            update = (main * half_way - slope * twice) * jnp.sqrt(scalings[j])
            update_ref[s] = update
            stats_ref[s, 0:1, :] = jnp.broadcast_to(traces[j], (1, 128))
            stats_ref[s, 1:2, :] = jnp.broadcast_to(total(update * update), (1, 128))
            stats_ref[s, 2:3, :] = jnp.broadcast_to(scalings[j], (1, 128))
            stats_ref[s, 3:8, :] = jnp.zeros((5, 128), jnp.float32)
        return carry

    lax.fori_loop(0, chunks, step, 0)

    for a in range(chunks):
        core_og(a).wait_send()
        for k in range(2):
            if a > 0:
                x_og(a, k).wait_send()
            z_og(a, k).wait_send()
    for j in range(features):
        core_act(j).wait_send()
        y_act(j).wait_send()
        f_act(j, 0).wait_send()
        f_act(j, 1).wait_send()


def gathered_updates(og, act):
    shard, rows = og.shape[0], og.shape[1] // lax.axis_size("dp")
    tokens, width = shard * lax.axis_size("dp"), act.shape[1]
    chunks, features = rows // BLK, width // BLK
    blocks = chunks * features
    outside = pl.BlockSpec(memory_space=pltpu.HBM)
    one = pltpu.SemaphoreType.DMA((chunks,))
    two = pltpu.SemaphoreType.DMA((chunks, 2))
    act_one = pltpu.SemaphoreType.DMA((features,))
    act_two = pltpu.SemaphoreType.DMA((features, 2))
    return pl.pallas_call(
        gather_kernel,
        in_specs=[outside, outside],
        out_specs=[pl.BlockSpec(memory_space=pltpu.VMEM)] * 3,
        out_shape=[
            pltpu.VMEM((blocks, BLK, BLK), jnp.float32),
            pltpu.VMEM((blocks, BLK, BLK), jnp.float32),
            pltpu.VMEM((blocks, 8, 128), jnp.float32),
        ],
        scratch_shapes=[
            pltpu.VMEM((chunks, tokens, BLK), jnp.bfloat16),
            pltpu.VMEM((features, tokens, BLK), jnp.bfloat16),
            pltpu.VMEM((features, 2, BLK, BLK), jnp.bfloat16),
            pltpu.VMEM((features, 2, BLK, BLK), jnp.bfloat16),
            one, one, one, two, two, two, two,
            act_one, act_one, act_one, act_one, act_one, act_one, act_one, act_two, act_two,
        ],
        compiler_params=pltpu.CompilerParams(
            collective_id=0, has_side_effects=True, vmem_limit_bytes=36 * 2**20
        ),
    )(og, act)


def finish_kernel(counts_ref, stats_ref, left_ref, update_in, update_ref, squares_ref, coupled_ref):
    del update_in
    features = counts_ref.shape[1]
    squares_ref[...] = jnp.zeros_like(squares_ref)

    def step(s, carry):
        a, j = lax.div(s, features), lax.rem(s, features)
        count = counts_ref[a, j]
        squares_ref[0:8, :] += jnp.broadcast_to(stats_ref[s, 0:1, :], (8, 128))

        @pl.when(count <= 1)
        def _():
            squares_ref[8:16, :] += jnp.broadcast_to(stats_ref[s, 1:2, :], (8, 128))

        @pl.when(count > 1)
        def _():
            coupled_ref[...] = stats_ref[s, 2:3, 0:1] * (left_ref[s] + SHIFT * identity())
            later_iterations(count, coupled_ref, update_ref.at[s])
            u = update_ref[s]
            squares_ref[8:16, :] += jnp.broadcast_to(total(u * u), (8, 128))

        return carry

    lax.fori_loop(0, counts_ref.shape[0] * features, step, 0)


def finished_updates(counts, stats, left, updates):
    vmem = pl.BlockSpec(memory_space=pltpu.VMEM)
    return pl.pallas_call(
        finish_kernel,
        in_specs=[pl.BlockSpec(memory_space=pltpu.SMEM), vmem, vmem, vmem],
        out_specs=[vmem, vmem],
        out_shape=[
            pltpu.VMEM(updates.shape, jnp.float32),
            pltpu.VMEM((16, 128), jnp.float32),
        ],
        scratch_shapes=[pltpu.VMEM((BLK, BLK), jnp.float32)],
        input_output_aliases={3: 0},
        compiler_params=pltpu.CompilerParams(vmem_limit_bytes=36 * 2**20),
    )(counts, stats, left, updates)


def ratio_kernel(groups, squares_ref, ratio_ref, *scratch):
    count = len(groups)
    buffers, sends, recvs = scratch[:count], scratch[count:2 * count], scratch[2 * count:]

    def place(group):
        index = 0
        for name, size in group:
            index = index * size + lax.axis_index(name)
        return index

    def device(group, index):
        found = {}
        for name, size in reversed(group):
            found[name] = lax.rem(index, size)
            index = lax.div(index, size)
        return found

    barrier = pltpu.get_barrier_semaphore()
    partners = 0
    for group in groups:
        extent = math.prod(size for _, size in group)
        for step in range(1, extent):
            pl.semaphore_signal(
                barrier, inc=1, device_id=device(group, lax.rem(place(group) + step, extent)),
                device_id_type=pl.DeviceIdType.MESH,
            )
            partners += 1
    pl.semaphore_wait(barrier, partners)
    sums = squares_ref[...]
    for group, buffer, send, recv in zip(groups, buffers, sends, recvs):
        me, extent = place(group), buffer.shape[0]
        buffer[me] = sums
        copies = []
        for step in range(1, extent):
            copy = remote(
                buffer.at[me], buffer.at[me], send.at[step - 1], recv.at[step - 1],
                **device(group, lax.rem(me + step, extent)),
            )
            copy.start()
            copies.append(copy)
        for copy in copies:
            copy.wait()
        sums = buffer[0]
        for i in range(1, extent):
            sums = sums + buffer[i]
    ratio_ref[...] = jnp.sqrt(sums[0:8, :] / sums[8:16, :])


def graft_ratio(squares):
    sizes = {name: lax.axis_size(name) for name in ("dp", "prec", "pair")}
    groups = [[("dp", sizes["dp"])], [("prec", sizes["prec"]), ("pair", sizes["pair"])]]
    extents = [math.prod(size for _, size in group) for group in groups]
    vmem = pl.BlockSpec(memory_space=pltpu.VMEM)
    sems = [pltpu.SemaphoreType.DMA((max(extent - 1, 1),)) for extent in extents]
    return pl.pallas_call(
        functools.partial(ratio_kernel, groups),
        in_specs=[vmem],
        out_specs=vmem,
        out_shape=jax.ShapeDtypeStruct((8, 128), jnp.float32),
        scratch_shapes=[pltpu.VMEM((extent, 16, 128), jnp.float32) for extent in extents] + sems + sems,
        compiler_params=pltpu.CompilerParams(
            collective_id=1, has_side_effects=True, vmem_limit_bytes=8 * 2**20
        ),
    )(squares)


def scale_kernel(ratio_ref, update_ref, out_ref):
    out_ref[...] = update_ref[...] * ratio_ref[0:1, 0:1]


def scaled_updates(ratio, updates):
    rows, width = updates.shape
    block = pl.BlockSpec((BLK // 2, width), lambda i: (i, 0))
    return pl.pallas_call(
        scale_kernel,
        grid=(rows // (BLK // 2),),
        in_specs=[pl.BlockSpec(memory_space=pltpu.VMEM), block],
        out_specs=block,
        out_shape=jax.ShapeDtypeStruct(updates.shape, jnp.float32),
        compiler_params=pltpu.CompilerParams(vmem_limit_bytes=48 * 2**20),
    )(ratio, updates)


def scale_blocks_kernel(ratio_ref, update_ref, out_ref, scaled, sem):
    features = out_ref.shape[1] // BLK

    def place(s):
        a, j = lax.div(s, features), lax.rem(s, features)
        there = out_ref.at[
            pl.ds(pl.multiple_of(a * BLK, BLK), BLK), pl.ds(pl.multiple_of(j * BLK, BLK), BLK)
        ]
        return pltpu.make_async_copy(scaled.at[s], there, sem.at[s])

    def scale(s, carry):
        scaled[s] = update_ref[s] * ratio_ref[0:1, 0:1]
        place(s).start()
        return carry

    def wait(s, carry):
        place(s).wait()
        return carry

    lax.fori_loop(0, scaled.shape[0], scale, 0)
    lax.fori_loop(0, scaled.shape[0], wait, 0)


def scaled_blocks(ratio, updates, shape):
    vmem = pl.BlockSpec(memory_space=pltpu.VMEM)
    return pl.pallas_call(
        scale_blocks_kernel,
        in_specs=[vmem, vmem],
        out_specs=pl.BlockSpec(memory_space=pl.ANY),
        out_shape=jax.ShapeDtypeStruct(shape, jnp.float32),
        scratch_shapes=[
            pltpu.VMEM(updates.shape, jnp.float32),
            pltpu.SemaphoreType.DMA((updates.shape[0],)),
        ],
        compiler_params=pltpu.CompilerParams(vmem_limit_bytes=36 * 2**20),
    )(ratio, updates)


def gathered_first(activations, output_grads, iter_counts):
    act = lax.all_gather(activations, "dp", axis=0, tiled=True)
    og = lax.all_to_all(output_grads, "dp", split_axis=1, concat_axis=0, tiled=True)
    return local_updates(og, act, iter_counts)


def per_device(activations, output_grads, iter_counts):
    sizes = [lax.axis_size(name) for name in ("dp", "prec", "pair")]
    if sizes[0] == 4 and sizes[1] % 2 == 0 and sizes[2] == 2:
        updates, left, stats = gathered_updates(output_grads, activations)
        updates, squares = finished_updates(iter_counts, stats, left, updates)
        shape = (output_grads.shape[1] // sizes[0], activations.shape[1])
        return scaled_blocks(graft_ratio(squares), updates, shape)
    updates, squares = gathered_first(activations, output_grads, iter_counts)
    return scaled_updates(graft_ratio(squares), updates)


def solution(mesh):
    in_specs = (P("dp", "prec"), P("dp", "pair"), P(("pair", "dp"), "prec"))
    out_specs = P(("pair", "dp"), "prec")
    return jax.shard_map(
        per_device, mesh=mesh, in_specs=in_specs, out_specs=out_specs, check_vma=False
    )
```
